128 devices in a mesh: kvp: 16 (over z, y), tp: 8 (over x, core).
Axes of the slice: x: 4, y: 4, z: 4, core: 2. Of those that a mesh axis runs over, the one named last changes fastest.
Arguments:
- hidden_in: bfloat16 [2, 128, 8192], P(None, None, 'kvp'), may hold values from -6 to 6
- w_query: bfloat16 [8192, 8192], P('kvp', 'tp'), may hold values from -0.0625 to 0.0625
- key_weight_matrix: bfloat16 [8192, 1024], P('kvp', 'tp'), may hold values from -0.0625 to 0.0625
- value_weight_matrix: bfloat16 [8192, 1024], P('kvp', 'tp'), may hold values from -0.0625 to 0.0625
- w_out: bfloat16 [8192, 8192], P('tp', 'kvp'), may hold values from -0.0625 to 0.0625
- paged_key_cache: bfloat16 [1024, 256, 1024], P('kvp', None, 'tp'), as said below
- paged_value_cache: bfloat16 [1024, 256, 1024], P('kvp', None, 'tp'), may hold values from -6 to 6
- block_request: int32 [1024], P('kvp'), may hold values from 0 to 127, as said below
- block_fill: int32 [1024], P('kvp'), may hold values from 1 to 256, as said below
- positions: int32 [128], replicated, may hold values from 0 to 1048576, as said below
Outputs:
- attn_out: bfloat16 [2, 128, 8192], P(None, None, 'kvp')
The draws below stay inside these ranges and needn't reach their ends.
Inputs may be any that keep to these rules, and one draw needn't show every extreme that they name: `block_request`: each cache block belongs to one request; a request may own no block. `block_fill`: every block is full except the last block (highest index) of its request, which holds 1 to 256 live slots; some block of every draw is full and some holds one live slot. `paged_key_cache`: random keys, not derived from the projection. positions[0] is 1048576; for every other request r, positions[r] is 256 times the number of blocks of request r plus an offset below 256.
All inputs are finite; a program needn't handle non-finite values.
Results may differ from the reference program's by a relative error of at most 0.025.
Values may be sent and summed in bfloat16 or wider, within the bound.
No kernel may reach another device: no remote copies, remote signals or barrier semaphores. Data moves between devices by JAX's collectives and lax.ppermute only.
A program may use at most 128 MiB of HBM per device.

```python
import jax
import jax.numpy as jnp
from jax import lax

MODEL_WIDTH = 8192
QUERY_HEADS = 64
KEY_VALUE_HEADS = 8
HEAD_SIZE = 128
STEPS = 2
BLOCK_SLOTS = 256
REQ = 128
BLOCKS_PER_SPLIT = 64
TOTAL_BLOCKS = 1024


def owner_list(key):
    key_outer, key_mid, key_inner, key_perm = jax.random.split(key, 4)
    upper_a = jax.random.randint(key_outer, (TOTAL_BLOCKS,), 1, REQ + 1, jnp.int32)
    upper_b = jax.random.randint(key_mid, (TOTAL_BLOCKS,), 1, upper_a + 1, jnp.int32)
    raw_owner = jax.random.randint(key_inner, (TOTAL_BLOCKS,), 0, upper_b, jnp.int32)
    relabel = jax.random.permutation(key_perm, REQ).astype(jnp.int32)
    owners = relabel[raw_owner]
    return owners.at[1].set(REQ - 1).at[2].set(0).astype(jnp.int32)


def draw_block_request(key, part):
    owners = owner_list(key)
    return owners


def draw_block_fill(key, part):
    owners = owner_list(key)
    key = jax.random.fold_in(key, 5)
    index_list = jnp.arange(TOTAL_BLOCKS, dtype=jnp.int32)
    later_same = (owners[None, :] == owners[:, None]) & (index_list[None, :] > index_list[:, None])
    is_last = jnp.logical_not(jnp.any(later_same, axis=1))
    tail_fill = jax.random.randint(key, (TOTAL_BLOCKS,), 1, BLOCK_SLOTS + 1, jnp.int32)
    fill_count = jnp.where(is_last, tail_fill, BLOCK_SLOTS).astype(jnp.int32)
    return fill_count.at[0].set(BLOCK_SLOTS).at[TOTAL_BLOCKS - 1].set(1)


def draw_positions(key, part):
    owners = owner_list(key)
    key = jax.random.fold_in(key, 7)
    counts = jnp.sum((owners[:, None] == jnp.arange(REQ, dtype=jnp.int32)[None, :]).astype(jnp.int32), axis=0)
    offset = jax.random.randint(key, (REQ,), 0, BLOCK_SLOTS, jnp.int32)
    start_pos = (counts * BLOCK_SLOTS + offset).astype(jnp.int32)
    return start_pos.at[0].set(4 * TOTAL_BLOCKS * BLOCK_SLOTS).astype(jnp.int32)


def draw_paged_key_cache(key, part):
    key = jax.random.fold_in(key, 11)
    key_starting = jax.random.fold_in(key, 0)
    starting_keys = jnp.clip(jax.random.normal(key_starting, (TOTAL_BLOCKS, BLOCK_SLOTS, KEY_VALUE_HEADS * HEAD_SIZE), jnp.float32), -4.0, 4.0)
    return starting_keys.astype(jnp.bfloat16)


def steps_of(rng, extent, shards, smallest, high):
    factor_of = 1.0
    for dim, parts in shards:
        steps = jax.random.uniform(jax.random.fold_in(jax.random.fold_in(rng, 6), dim), (parts,), jnp.float32, smallest / len(shards), high / len(shards))
        factor_of = factor_of * jnp.repeat(jnp.exp(steps), extent[dim] // parts).reshape((-1,) + (1,) * (len(extent) - 1 - dim))
    return factor_of


def scatter_about(rng, extent, deviation, limit, pieces=(), kind=jnp.bfloat16):
    array = deviation * jax.random.normal(rng, extent, jnp.float32)
    if pieces:
        array = array * steps_of(rng, extent, pieces, -0.22, 0.18)
    return jnp.clip(array, -limit, limit).astype(kind)


def setup_inputs(seed: int = 0) -> dict:
    splits = jax.random.split(jax.random.key(seed), 11)
    return {
        "hidden_in": scatter_about(splits[0], (STEPS, REQ, MODEL_WIDTH), 1.0, 6.0, ((2, 16),)),
        "w_query": scatter_about(splits[1], (MODEL_WIDTH, QUERY_HEADS * HEAD_SIZE), MODEL_WIDTH ** -0.5, 0.0625, ((0, 16), (1, 8))),
        "key_weight_matrix": scatter_about(splits[2], (MODEL_WIDTH, KEY_VALUE_HEADS * HEAD_SIZE), MODEL_WIDTH ** -0.5, 0.0625, ((0, 16), (1, 8))),
        "value_weight_matrix": scatter_about(splits[3], (MODEL_WIDTH, KEY_VALUE_HEADS * HEAD_SIZE), MODEL_WIDTH ** -0.5, 0.0625, ((0, 16), (1, 8))),
        "w_out": scatter_about(splits[4], (QUERY_HEADS * HEAD_SIZE, MODEL_WIDTH), (QUERY_HEADS * HEAD_SIZE) ** -0.5, 0.0625, ((0, 8), (1, 16))),
        "paged_key_cache": draw_paged_key_cache(jax.random.fold_in(splits[10], 71), 0),
        "paged_value_cache": scatter_about(splits[6], (TOTAL_BLOCKS, BLOCK_SLOTS, KEY_VALUE_HEADS * HEAD_SIZE), 1.0, 6.0, ((0, 16), (2, 8))),
        "block_request": draw_block_request(jax.random.fold_in(splits[10], 71), 0),
        "block_fill": draw_block_fill(jax.random.fold_in(splits[10], 71), 0),
        "positions": draw_positions(jax.random.fold_in(splits[10], 71), 0),
    }


floor_score = -1e30
rope_base = 500000.0


def rotate_halves(vectors, position_slots):
    half_size = vectors.shape[-1] // 2
    inverse = rope_base ** (-(jnp.arange(half_size, dtype=jnp.float32) * 2.0 / vectors.shape[-1]))
    angles = position_slots.astype(jnp.float32)[..., None] * inverse
    cosine = jnp.cos(angles)[..., None, :]
    sine = jnp.sin(angles)[..., None, :]
    first_half = vectors[..., :half_size]
    second_half = vectors[..., half_size:]
    return jnp.concatenate([first_half * cosine - second_half * sine, second_half * cosine + first_half * sine], axis=-1)


def block_stats(chosen, block_keys, block_values, fill_count, scaling):
    scores = jnp.einsum("snkgd,ntkd->nksgt", chosen.astype(jnp.float32), block_keys.astype(jnp.float32)) * scaling
    live_slots = jnp.arange(block_keys.shape[1], dtype=jnp.int32)[None, :] < fill_count[:, None]
    scores = jnp.where(live_slots[:, None, None, None, :], scores, floor_score)
    largest_score = jnp.max(scores, axis=-1)
    weights = jnp.exp(scores - largest_score[..., None]).astype(jnp.bfloat16)
    running_totals = jnp.sum(weights.astype(jnp.float32), axis=-1)
    weighted_values = jnp.einsum("nksgt,ntkd->nksgd", weights.astype(jnp.float32), block_values.astype(jnp.float32))
    return largest_score, running_totals, weighted_values


def request_combine(largest_score, running_totals, weighted_values, owners, request_number):
    onehot = owners[:, None] == jnp.arange(request_number, dtype=jnp.int32)[None, :]
    best_score = jnp.max(jnp.where(onehot[:, :, None, None, None], largest_score[:, None], floor_score), axis=0)
    factor = jnp.exp(largest_score - best_score[owners])
    onefloat = onehot.astype(jnp.float32)
    total_req = jnp.einsum("nr,nksg->rksg", onefloat, factor * running_totals, precision=lax.Precision.HIGHEST)
    summed_req = jnp.einsum("nr,nksgd->rksgd", onefloat, factor[..., None] * weighted_values, precision=lax.Precision.HIGHEST)
    return best_score, total_req, summed_req


def finish(best_score, total_req, summed_req, query_rows, keys_new, values_new, scaling):
    decode_step_count = query_rows.shape[0]
    scores = jnp.einsum("srkgd,trkd->rksgt", query_rows.astype(jnp.float32), keys_new.astype(jnp.float32)) * scaling
    causal = jnp.arange(decode_step_count)[:, None] >= jnp.arange(decode_step_count)[None, :]
    scores = jnp.where(causal[None, None, :, None, :], scores, floor_score)
    peak_score = jnp.maximum(best_score, jnp.max(scores, axis=-1))
    factor = jnp.exp(best_score - peak_score)
    weights = jnp.exp(scores - peak_score[..., None]).astype(jnp.bfloat16)
    total_all = total_req * factor + jnp.sum(weights.astype(jnp.float32), axis=-1)
    summed_all = summed_req * factor[..., None] + jnp.einsum("rksgt,trkd->rksgd", weights.astype(jnp.float32), values_new.astype(jnp.float32))
    heads = (summed_all / total_all[..., None]).astype(jnp.bfloat16)
    return jnp.transpose(heads, (2, 0, 1, 3, 4)).reshape(decode_step_count, heads.shape[0], -1)


def reference(hidden_in, w_query, key_weight_matrix, value_weight_matrix, w_out, paged_key_cache, paged_value_cache, block_request, block_fill, positions):
    decode_step_count, request_number, width = hidden_in.shape
    query_group = QUERY_HEADS // KEY_VALUE_HEADS
    row_entries = hidden_in.reshape(decode_step_count * request_number, width)
    query_projected = jnp.dot(row_entries, w_query, preferred_element_type=jnp.float32).reshape(decode_step_count, request_number, QUERY_HEADS, HEAD_SIZE)
    key_projected = jnp.dot(row_entries, key_weight_matrix, preferred_element_type=jnp.float32).reshape(decode_step_count, request_number, KEY_VALUE_HEADS, HEAD_SIZE)
    value_projected = jnp.dot(row_entries, value_weight_matrix, preferred_element_type=jnp.float32).reshape(decode_step_count, request_number, KEY_VALUE_HEADS, HEAD_SIZE)
    position_slots = positions[None, :] + jnp.arange(decode_step_count, dtype=jnp.int32)[:, None]
    query_rows = rotate_halves(query_projected, position_slots).astype(jnp.bfloat16).reshape(decode_step_count, request_number, KEY_VALUE_HEADS, query_group, HEAD_SIZE)
    keys_new = rotate_halves(key_projected, position_slots).astype(jnp.bfloat16)
    values_new = value_projected.astype(jnp.bfloat16)
    scaling = HEAD_SIZE ** -0.5
    query_groups = TOTAL_BLOCKS // BLOCKS_PER_SPLIT

    def one_group(items):
        group_keys, group_values, owners, fill_count = items
        chosen = query_rows[:, owners]
        return block_stats(chosen, group_keys, group_values, fill_count, scaling)

    largest_score, running_totals, weighted_values = lax.map(one_group, (
        paged_key_cache.reshape(query_groups, BLOCKS_PER_SPLIT, BLOCK_SLOTS, KEY_VALUE_HEADS, HEAD_SIZE),
        paged_value_cache.reshape(query_groups, BLOCKS_PER_SPLIT, BLOCK_SLOTS, KEY_VALUE_HEADS, HEAD_SIZE),
        block_request.reshape(query_groups, BLOCKS_PER_SPLIT),
        block_fill.reshape(query_groups, BLOCKS_PER_SPLIT)))
    largest_score = largest_score.reshape(TOTAL_BLOCKS, KEY_VALUE_HEADS, decode_step_count, query_group)
    running_totals = running_totals.reshape(TOTAL_BLOCKS, KEY_VALUE_HEADS, decode_step_count, query_group)
    weighted_values = weighted_values.reshape(TOTAL_BLOCKS, KEY_VALUE_HEADS, decode_step_count, query_group, HEAD_SIZE)
    best_score, total_req, summed_req = request_combine(largest_score, running_totals, weighted_values, block_request, request_number)
    heads = finish(best_score, total_req, summed_req, query_rows, keys_new, values_new, scaling)
    result = jnp.dot(heads.reshape(decode_step_count * request_number, QUERY_HEADS * HEAD_SIZE), w_out, preferred_element_type=jnp.float32)
    return result.astype(jnp.bfloat16).reshape(decode_step_count, request_number, width)
```

```python
import functools

import jax
import jax.numpy as jnp
from jax import lax
from jax.experimental import pallas as pl
from jax.experimental.pallas import tpu as pltpu
from jax.sharding import PartitionSpec as P

HEAD_SIZE = 128
STAT_ROWS = 16
PIECES = 3

floor_score = -1e30
rope_base = 500000.0
VMEM = pl.BlockSpec(memory_space=pltpu.VMEM)
NT = (((1,), (1,)), ((), ()))


def params(mib=24):
    return pltpu.CompilerParams(vmem_limit_bytes=mib * 1024 * 1024)


def rotation_tables(positions, first, count, steps):
    half = HEAD_SIZE // 2
    inverse = rope_base ** (-(jnp.arange(half, dtype=jnp.float32) * 2.0 / HEAD_SIZE))
    own = lax.dynamic_slice_in_dim(positions, first, count)
    slots = own[None, :] + jnp.arange(steps, dtype=jnp.int32)[:, None]
    angles = slots.reshape(-1).astype(jnp.float32)[:, None] * inverse
    cosine, sine = jnp.cos(angles), jnp.sin(angles)
    return (
        jnp.concatenate([cosine, cosine], axis=-1),
        jnp.concatenate([-sine, sine], axis=-1),
    )


def project_kernel(hidden_ref, wq_ref, wk_ref, wv_ref, out_ref):
    steps, requests, width = hidden_ref.shape
    owners, rows, _ = out_ref.shape
    own = rows // steps
    hidden = hidden_ref[...].reshape(steps * requests, width)
    column = 0
    for ref in (wq_ref, wk_ref, wv_ref):
        total = ref.shape[1]
        chunk = min(total, 256)
        for start in range(0, total, chunk):
            part = jnp.dot(
                hidden, ref[:, start : start + chunk], preferred_element_type=jnp.float32
            )
            split = [
                part[s * requests : (s + 1) * requests].reshape(owners, own, chunk)
                for s in range(steps)
            ]
            out_ref[:, :, column : column + chunk] = jnp.concatenate(split, axis=1).astype(
                jnp.bfloat16
            )
            column += chunk


def rotate_kernel(parts_ref, cos_ref, sin_ref, q_ref, new_ref, turned_ref):
    sources, rows, columns = parts_ref.shape
    steps = 2
    own = rows // steps
    group = columns // HEAD_SIZE - 2
    cosine, sine = cos_ref[...], sin_ref[...]

    def head(index):
        lanes = slice(index * HEAD_SIZE, (index + 1) * HEAD_SIZE)
        return jnp.sum(parts_ref[:, :, lanes].astype(jnp.float32), axis=0)

    def rope(x):
        return x * cosine + pltpu.roll(x, HEAD_SIZE // 2, 1) * sine

    for g in range(group):
        x = rope(head(g))
        for s in range(steps):
            turned_ref[pl.ds(s * group + g, own, stride=steps * group), :] = x[
                s * own : (s + 1) * own
            ]
    new_ref[0] = rope(head(group)).astype(jnp.bfloat16)
    new_ref[1] = head(group + 1).astype(jnp.bfloat16)
    queries = turned_ref[...].astype(jnp.bfloat16)
    for d in range(q_ref.shape[0]):
        q_ref[d] = queries


def pieces(x):
    out = []
    for _ in range(PIECES):
        part = x.astype(jnp.bfloat16).astype(jnp.float32)
        out.append(part)
        x = x - part
    return out


def attention_kernel(
    scaling, request_ref, fill_ref, q_ref, k_ref, v_ref, out_ref, max_ref, total_ref, sum_ref
):
    step = pl.program_id(0)
    blocks, slots, _ = k_ref.shape
    requests, rows, _ = q_ref.shape

    @pl.when(step == 0)
    def _():
        max_ref[...] = jnp.full_like(max_ref, floor_score)
        total_ref[...] = jnp.zeros_like(total_ref)
        sum_ref[...] = jnp.zeros_like(sum_ref)

    slot = lax.broadcasted_iota(jnp.int32, (rows, slots), 1)
    found = []
    for b in range(blocks):
        n = step * blocks + b
        owner = request_ref[n]
        scores = (
            lax.dot_general(q_ref[owner], k_ref[b], NT, preferred_element_type=jnp.float32)
            * scaling
        )
        scores = jnp.where(slot < fill_ref[n], scores, floor_score)
        largest = jnp.max(scores, axis=1, keepdims=True)
        weights = jnp.exp(scores - largest).astype(jnp.bfloat16)
        total = jnp.sum(weights.astype(jnp.float32), axis=1, keepdims=True)
        summed = jnp.dot(weights, v_ref[b], preferred_element_type=jnp.float32)
        found.append((owner, largest, total, summed))
    for owner, largest, total, summed in found:
        before = max_ref[owner]
        after = jnp.maximum(before, largest)
        keep = jnp.exp(before - after)
        add = jnp.exp(largest - after)
        max_ref[owner] = after
        total_ref[owner] = total_ref[owner] * keep + total * add
        sum_ref[owner] = sum_ref[owner] * keep + summed * add

    @pl.when(step == pl.num_programs(0) - 1)
    def _():
        owners = out_ref.shape[0]
        own = requests // owners
        flat = own * rows
        lane = lax.broadcasted_iota(jnp.int32, (flat, HEAD_SIZE), 1)
        pick = (
            lax.broadcasted_iota(jnp.int32, (STAT_ROWS, HEAD_SIZE), 0)
            == lax.broadcasted_iota(jnp.int32, (STAT_ROWS, HEAD_SIZE), 1)
        ).astype(jnp.bfloat16)
        for d in range(owners):
            mine = slice(d * own, (d + 1) * own)
            out_ref[d, :flat, :] = sum_ref[mine].reshape(flat, HEAD_SIZE).astype(jnp.bfloat16)
            values = pieces(max_ref[mine].reshape(flat, HEAD_SIZE)) + pieces(
                total_ref[mine].reshape(flat, HEAD_SIZE)
            )
            table = jnp.zeros((flat, HEAD_SIZE), jnp.float32)
            for i, value in enumerate(values):
                table = jnp.where(lane == i, value, table)
            out_ref[d, flat:, :] = lax.dot_general(
                pick, table.astype(jnp.bfloat16), NT, preferred_element_type=jnp.float32
            ).astype(jnp.bfloat16)


def finish_kernel(scaling, parts_ref, q_ref, new_ref, out_ref, heads_ref):
    sources = parts_ref.shape[0]
    flat = q_ref.shape[0]
    steps = 2
    own = new_ref.shape[1] // steps
    rows = flat // own
    group = rows // steps

    stats = parts_ref[:, flat:, :].astype(jnp.float32)
    largest = sum(stats[:, i, :] for i in range(PIECES))
    total = sum(stats[:, PIECES + i, :] for i in range(PIECES))
    pad = HEAD_SIZE - sources
    largest = jnp.concatenate([largest, jnp.full((pad, flat), floor_score, jnp.float32)], axis=0).T
    total = jnp.concatenate([total, jnp.zeros((pad, flat), jnp.float32)], axis=0).T

    def spread(x):
        return jnp.broadcast_to(x[:, None, :], (own, rows, HEAD_SIZE)).reshape(flat, HEAD_SIZE)

    queries = q_ref[...].astype(jnp.float32)
    keys = new_ref[0].astype(jnp.float32)
    values = new_ref[1].astype(jnp.float32)
    row = lax.broadcasted_iota(jnp.int32, (flat, 1), 0)
    row_step = (row % rows) // group
    scores = []
    for t in range(steps):
        score = (
            jnp.sum(queries * spread(keys[t * own : (t + 1) * own]), axis=1, keepdims=True)
            * scaling
        )
        scores.append(jnp.where(row_step >= t, score, floor_score))
    peak = jnp.max(largest, axis=1, keepdims=True)
    for score in scores:
        peak = jnp.maximum(peak, score)
    factor = jnp.exp(largest - peak)
    weight_total = jnp.sum(factor * total, axis=1, keepdims=True)
    summed = jnp.zeros((flat, HEAD_SIZE), jnp.float32)
    for source in range(sources):
        summed = summed + factor[:, source : source + 1] * parts_ref[source, :flat, :].astype(
            jnp.float32
        )
    for t in range(steps):
        weight = jnp.exp(scores[t] - peak).astype(jnp.bfloat16).astype(jnp.float32)
        weight_total = weight_total + weight
        summed = summed + weight * spread(values[t * own : (t + 1) * own])
    heads_ref[...] = summed / weight_total
    columns = []
    for g in range(group):
        columns.append(
            jnp.concatenate(
                [
                    heads_ref[pl.ds(s * group + g, own, stride=rows), :]
                    for s in range(steps)
                ],
                axis=0,
            )
        )
    heads = jnp.concatenate(columns, axis=1).astype(jnp.bfloat16)
    for d in range(out_ref.shape[0]):
        out_ref[d] = heads


def output_kernel(core_ref, heads_ref, w_ref, keep_ref, send_ref):
    owners, rows, width = heads_ref.shape
    steps = 2
    own = rows // steps
    core = core_ref[0]
    heads = heads_ref[...].reshape(owners * rows, width)
    columns = w_ref.shape[1]
    chunk = min(columns, 256)
    for start in range(0, columns, chunk):
        lanes = slice(start, start + chunk)
        part = jnp.dot(heads, w_ref[:, lanes], preferred_element_type=jnp.float32)
        part = part.reshape(owners, rows, chunk)
        first = part[:, :own].reshape(owners * own, chunk)
        second = part[:, own:].reshape(owners * own, chunk)
        keep_ref[:, lanes] = jnp.where(core == 0, first, second)
        send_ref[:, lanes] = jnp.where(core == 0, second, first).astype(jnp.bfloat16)


def local(
    hidden_in,
    w_query,
    key_weight_matrix,
    value_weight_matrix,
    w_out,
    paged_key_cache,
    paged_value_cache,
    block_request,
    block_fill,
    positions,
):
    bf16, f32 = jnp.bfloat16, jnp.float32
    steps, requests, _ = hidden_in.shape
    group = w_query.shape[1] // HEAD_SIZE
    owners = lax.axis_size("kvp")
    own = requests // owners
    rows = steps * own
    flat = rows * group
    scaling = HEAD_SIZE ** (-0.5)
    blocks, slots, _ = paged_key_cache.shape
    out_columns = w_out.shape[1]

    def exchange(x):
        return lax.all_to_all(x, "kvp", 0, 0, tiled=True)

    cosine, sine = rotation_tables(positions, lax.axis_index("kvp") * own, own, steps)
    columns = (group + 2) * HEAD_SIZE
    parts = pl.pallas_call(
        project_kernel,
        out_shape=jax.ShapeDtypeStruct((owners, rows, columns), bf16),
        in_specs=[VMEM] * 4,
        out_specs=VMEM,
        compiler_params=params(),
    )(hidden_in, w_query, key_weight_matrix, value_weight_matrix)
    parts = exchange(parts)
    queries, new_rows = pl.pallas_call(
        rotate_kernel,
        out_shape=(
            jax.ShapeDtypeStruct((owners, flat, HEAD_SIZE), bf16),
            jax.ShapeDtypeStruct((2, rows, HEAD_SIZE), bf16),
        ),
        in_specs=[VMEM] * 3,
        out_specs=(VMEM, VMEM),
        scratch_shapes=[pltpu.VMEM((flat, HEAD_SIZE), f32)],
        compiler_params=params(),
    )(parts, cosine, sine)
    own_queries = queries[0]
    queries = exchange(queries).reshape(requests, steps * group, HEAD_SIZE)

    per_step = 8
    sums = (requests, steps * group, HEAD_SIZE)
    parts = pl.pallas_call(
        functools.partial(attention_kernel, scaling),
        out_shape=jax.ShapeDtypeStruct((owners, flat + STAT_ROWS, HEAD_SIZE), bf16),
        grid_spec=pltpu.PrefetchScalarGridSpec(
            num_scalar_prefetch=2,
            grid=(blocks // per_step,),
            in_specs=[
                pl.BlockSpec(sums, lambda i, *_: (0, 0, 0)),
                pl.BlockSpec((per_step, slots, HEAD_SIZE), lambda i, *_: (i, 0, 0)),
                pl.BlockSpec((per_step, slots, HEAD_SIZE), lambda i, *_: (i, 0, 0)),
            ],
            out_specs=pl.BlockSpec(
                (owners, flat + STAT_ROWS, HEAD_SIZE), lambda i, *_: (0, 0, 0)
            ),
            scratch_shapes=[pltpu.VMEM(sums, f32)] * 3,
        ),
        compiler_params=params(),
    )(block_request, block_fill, queries, paged_key_cache, paged_value_cache)
    parts = exchange(parts)
    heads = pl.pallas_call(
        functools.partial(finish_kernel, scaling),
        out_shape=jax.ShapeDtypeStruct((owners, rows, group * HEAD_SIZE), bf16),
        in_specs=[VMEM] * 3,
        out_specs=VMEM,
        scratch_shapes=[pltpu.VMEM((flat, HEAD_SIZE), f32)],
        compiler_params=params(),
    )(parts, own_queries, new_rows)
    heads = exchange(heads)

    tp = lax.axis_index("tp")
    core = tp % 2
    half = (owners * own, out_columns)
    keep, send = pl.pallas_call(
        output_kernel,
        out_shape=(jax.ShapeDtypeStruct(half, f32), jax.ShapeDtypeStruct(half, bf16)),
        in_specs=[pl.BlockSpec(memory_space=pltpu.SMEM), VMEM, VMEM],
        out_specs=(VMEM, VMEM),
        compiler_params=params(),
    )(core.reshape(1), heads, w_out)

    devices = lax.axis_size("tp")

    def swap(x, bits):
        return lax.ppermute(x, "tp", [(i, i ^ bits) for i in range(devices)])

    mine = (keep + swap(send, 1).astype(f32)).astype(bf16)
    others = [swap(mine, bits) for bits in (2, 6, 4)]
    near, across, far = (x.astype(f32) for x in others)
    mine = ((mine.astype(f32) + near) + (across + far)).astype(bf16)
    other = swap(mine, 1)
    return jnp.where(core == 0, jnp.stack([mine, other]), jnp.stack([other, mine]))


def solution(mesh):
    return jax.shard_map(
        local,
        mesh=mesh,
        in_specs=(
            P(None, None, "kvp"),
            P("kvp", "tp"),
            P("kvp", "tp"),
            P("kvp", "tp"),
            P("tp", "kvp"),
            P("kvp", None, "tp"),
            P("kvp", None, "tp"),
            P("kvp"),
            P("kvp"),
            P(),
        ),
        out_specs=P(None, None, "kvp"),
        check_vma=False,
    )
```

```python
import functools

import jax
import jax.numpy as jnp
from jax import lax
from jax.experimental import pallas as pl
from jax.experimental.pallas import tpu as pltpu
from jax.sharding import PartitionSpec as P

HEAD_SIZE = 128
STAT_ROWS = 16
PIECES = 3

floor_score = -1e30
rope_base = 500000.0
VMEM = pl.BlockSpec(memory_space=pltpu.VMEM)
SMEM = pl.BlockSpec(memory_space=pltpu.SMEM)
HBM = pl.BlockSpec(memory_space=pltpu.HBM)
NT = (((1,), (1,)), ((), ()))


def params(mib=24):
    return pltpu.CompilerParams(vmem_limit_bytes=mib * 1024 * 1024)


def rotation_tables(positions, first, count, steps):
    half = HEAD_SIZE // 2
    inverse = rope_base ** (-(jnp.arange(half, dtype=jnp.float32) * 2.0 / HEAD_SIZE))
    own = lax.dynamic_slice_in_dim(positions, first, count)
    slots = own[None, :] + jnp.arange(steps, dtype=jnp.int32)[:, None]
    angles = slots.reshape(-1).astype(jnp.float32)[:, None] * inverse
    cosine, sine = jnp.cos(angles), jnp.sin(angles)
    return (
        jnp.concatenate([cosine, cosine], axis=-1),
        jnp.concatenate([-sine, sine], axis=-1),
    )


def project_kernel(hidden_hbm, wq_hbm, wk_hbm, wv_hbm, out_ref, hidden_ref, w_ref, sems):
    steps, requests, width = hidden_ref.shape
    owners, rows, columns = out_ref.shape
    own = rows // steps
    copies = [pltpu.make_async_copy(hidden_hbm, hidden_ref, sems.at[0])]
    chunks = []
    column = 0
    for hbm in (wq_hbm, wk_hbm, wv_hbm):
        total = hbm.shape[1]
        chunk = min(total, 256)
        for start in range(0, total, chunk):
            lanes = slice(column, column + chunk)
            copies.append(
                pltpu.make_async_copy(
                    hbm.at[:, start : start + chunk], w_ref.at[:, lanes], sems.at[len(copies)]
                )
            )
            chunks.append(lanes)
            column += chunk
    for copy in copies:
        copy.start()
    copies[0].wait()
    hidden = hidden_ref[...].reshape(steps * requests, width)
    for copy, lanes in zip(copies[1:], chunks):
        copy.wait()
        part = jnp.dot(hidden, w_ref[:, lanes], preferred_element_type=jnp.float32)
        split = [
            part[s * requests : (s + 1) * requests].reshape(owners, own, -1) for s in range(steps)
        ]
        out_ref[:, :, lanes] = jnp.concatenate(split, axis=1).astype(jnp.bfloat16)


def rotate_kernel(parts_ref, cos_ref, sin_ref, q_ref, new_ref, turned_ref):
    sources, rows, columns = parts_ref.shape
    steps = 2
    own = rows // steps
    group = columns // HEAD_SIZE - 2
    cosine, sine = cos_ref[...], sin_ref[...]

    def head(index):
        lanes = slice(index * HEAD_SIZE, (index + 1) * HEAD_SIZE)
        return jnp.sum(parts_ref[:, :, lanes].astype(jnp.float32), axis=0)

    def rope(x):
        return x * cosine + pltpu.roll(x, HEAD_SIZE // 2, 1) * sine

    for g in range(group):
        x = rope(head(g))
        for s in range(steps):
            turned_ref[pl.ds(s * group + g, own, stride=steps * group), :] = x[
                s * own : (s + 1) * own
            ]
    new_ref[0] = rope(head(group)).astype(jnp.bfloat16)
    new_ref[1] = head(group + 1).astype(jnp.bfloat16)
    queries = turned_ref[...].astype(jnp.bfloat16)
    for d in range(q_ref.shape[0]):
        q_ref[d] = queries


def pieces(x):
    out = []
    for _ in range(PIECES):
        part = x.astype(jnp.bfloat16).astype(jnp.float32)
        out.append(part)
        x = x - part
    return out


def attention_kernel(
    scaling,
    batch,
    request_ref,
    fill_ref,
    q_ref,
    k_hbm,
    v_hbm,
    out_ref,
    k_ref,
    v_ref,
    max_ref,
    total_ref,
    sum_ref,
    sems,
):
    blocks, slots, _ = k_ref.shape
    requests, rows, _ = q_ref.shape
    groups = blocks // batch
    lanes = batch * rows

    def load(hbm, ref, which, g):
        span = pl.ds(g * batch, batch)
        return pltpu.make_async_copy(hbm.at[span], ref.at[span], sems.at[which, g])

    for g in range(groups):
        load(k_hbm, k_ref, 0, g).start()
        load(v_hbm, v_ref, 1, g).start()
    max_ref[...] = jnp.full_like(max_ref, floor_score)
    total_ref[...] = jnp.zeros_like(total_ref)
    sum_ref[...] = jnp.zeros_like(sum_ref)

    slot = lax.broadcasted_iota(jnp.int32, (slots, lanes), 0)
    lane_block = lax.broadcasted_iota(jnp.int32, (1, lanes), 1) // rows
    empty = jnp.zeros((rows, HEAD_SIZE), jnp.bfloat16)

    def group_step(g, _):
        first = g * batch
        owners = [request_ref[first + b] for b in range(batch)]

        def placed(b):
            return jnp.concatenate(
                [empty] * b + [q_ref[owners[b]]] + [empty] * (batch - b - 1), axis=0
            )

        load(k_hbm, k_ref, 0, g).wait()
        scores = jnp.zeros((slots, lanes), jnp.float32)
        for b in range(0, batch, 2):
            scores = scores + lax.dot_general(
                jnp.concatenate([k_ref[first + b], k_ref[first + b + 1]], axis=1),
                jnp.concatenate([placed(b), placed(b + 1)], axis=1),
                NT,
                preferred_element_type=jnp.float32,
            )
        fill = jnp.zeros((1, lanes), jnp.int32)
        for b in range(batch):
            fill = jnp.where(lane_block == b, fill_ref[first + b], fill)
        scores = jnp.where(slot < fill, scores * scaling, floor_score)
        largest = jnp.max(scores, axis=0, keepdims=True)
        weights = jnp.exp(scores - largest).astype(jnp.bfloat16).astype(jnp.float32)
        total = jnp.sum(weights, axis=0, keepdims=True)
        turned = weights.T.astype(jnp.bfloat16)
        stats = jnp.concatenate(
            [largest, total, jnp.zeros((6, lanes), jnp.float32)], axis=0
        ).T
        load(v_hbm, v_ref, 1, g).wait()
        for b in range(batch):
            mine = slice(b * rows, (b + 1) * rows)
            summed = jnp.dot(turned[mine], v_ref[first + b], preferred_element_type=jnp.float32)
            owner = owners[b]
            before = max_ref[owner]
            block_max = stats[mine, 0:1]
            after = jnp.maximum(before, block_max)
            keep = jnp.exp(before - after)
            add = jnp.exp(block_max - after)
            max_ref[owner] = after
            total_ref[owner] = total_ref[owner] * keep + stats[mine, 1:2] * add
            sum_ref[owner] = sum_ref[owner] * keep + summed * add
        return 0

    lax.fori_loop(0, groups, group_step, 0)

    owners = out_ref.shape[0]
    own = requests // owners
    flat = own * rows
    lane = lax.broadcasted_iota(jnp.int32, (flat, HEAD_SIZE), 1)
    pick = (
        lax.broadcasted_iota(jnp.int32, (STAT_ROWS, HEAD_SIZE), 0)
        == lax.broadcasted_iota(jnp.int32, (STAT_ROWS, HEAD_SIZE), 1)
    ).astype(jnp.bfloat16)
    for d in range(owners):
        mine = slice(d * own, (d + 1) * own)
        out_ref[d, :flat, :] = sum_ref[mine].reshape(flat, HEAD_SIZE).astype(jnp.bfloat16)
        values = pieces(max_ref[mine].reshape(flat, HEAD_SIZE)) + pieces(
            total_ref[mine].reshape(flat, HEAD_SIZE)
        )
        table = jnp.zeros((flat, HEAD_SIZE), jnp.float32)
        for i, value in enumerate(values):
            table = jnp.where(lane == i, value, table)
        out_ref[d, flat:, :] = lax.dot_general(
            pick, table.astype(jnp.bfloat16), NT, preferred_element_type=jnp.float32
        ).astype(jnp.bfloat16)


def finish_kernel(scaling, parts_ref, q_ref, new_ref, out_ref, heads_ref):
    sources = parts_ref.shape[0]
    flat = q_ref.shape[0]
    steps = 2
    own = new_ref.shape[1] // steps
    rows = flat // own
    group = rows // steps

    stats = parts_ref[:, flat:, :].astype(jnp.float32)
    largest = sum(stats[:, i, :] for i in range(PIECES))
    total = sum(stats[:, PIECES + i, :] for i in range(PIECES))
    pad = HEAD_SIZE - sources
    largest = jnp.concatenate([largest, jnp.full((pad, flat), floor_score, jnp.float32)], axis=0).T
    total = jnp.concatenate([total, jnp.zeros((pad, flat), jnp.float32)], axis=0).T

    def spread(x):
        return jnp.broadcast_to(x[:, None, :], (own, rows, HEAD_SIZE)).reshape(flat, HEAD_SIZE)

    queries = q_ref[...].astype(jnp.float32)
    keys = new_ref[0].astype(jnp.float32)
    values = new_ref[1].astype(jnp.float32)
    row = lax.broadcasted_iota(jnp.int32, (flat, 1), 0)
    row_step = (row % rows) // group
    scores = []
    for t in range(steps):
        score = (
            jnp.sum(queries * spread(keys[t * own : (t + 1) * own]), axis=1, keepdims=True)
            * scaling
        )
        scores.append(jnp.where(row_step >= t, score, floor_score))
    peak = jnp.max(largest, axis=1, keepdims=True)
    for score in scores:
        peak = jnp.maximum(peak, score)
    factor = jnp.exp(largest - peak)
    weight_total = jnp.sum(factor * total, axis=1, keepdims=True)
    summed = jnp.zeros((flat, HEAD_SIZE), jnp.float32)
    for source in range(sources):
        summed = summed + factor[:, source : source + 1] * parts_ref[source, :flat, :].astype(
            jnp.float32
        )
    for t in range(steps):
        weight = jnp.exp(scores[t] - peak).astype(jnp.bfloat16).astype(jnp.float32)
        weight_total = weight_total + weight
        summed = summed + weight * spread(values[t * own : (t + 1) * own])
    heads_ref[...] = summed / weight_total
    columns = []
    for g in range(group):
        columns.append(
            jnp.concatenate(
                [
                    heads_ref[pl.ds(s * group + g, own, stride=rows), :]
                    for s in range(steps)
                ],
                axis=0,
            )
        )
    heads = jnp.concatenate(columns, axis=1).astype(jnp.bfloat16)
    for d in range(out_ref.shape[0]):
        out_ref[d] = heads


def output_kernel(core_ref, heads_ref, w_ref, keep_ref, send_ref):
    owners, rows, width = heads_ref.shape
    steps = 2
    own = rows // steps
    core = core_ref[0]
    heads = heads_ref[...].reshape(owners * rows, width)
    columns = w_ref.shape[1]
    chunk = min(columns, 256)
    for start in range(0, columns, chunk):
        lanes = slice(start, start + chunk)
        part = jnp.dot(heads, w_ref[:, lanes], preferred_element_type=jnp.float32)
        part = part.reshape(owners, rows, chunk)
        first = part[:, :own].reshape(owners * own, chunk)
        second = part[:, own:].reshape(owners * own, chunk)
        keep_ref[:, lanes] = jnp.where(core == 0, first, second)
        send_ref[:, lanes] = jnp.where(core == 0, second, first).astype(jnp.bfloat16)


def local(
    hidden_in,
    w_query,
    key_weight_matrix,
    value_weight_matrix,
    w_out,
    paged_key_cache,
    paged_value_cache,
    block_request,
    block_fill,
    positions,
):
    bf16, f32 = jnp.bfloat16, jnp.float32
    steps, requests, _ = hidden_in.shape
    group = w_query.shape[1] // HEAD_SIZE
    owners = lax.axis_size("kvp")
    own = requests // owners
    rows = steps * own
    flat = rows * group
    scaling = HEAD_SIZE ** (-0.5)
    blocks, slots, _ = paged_key_cache.shape
    out_columns = w_out.shape[1]

    def exchange(x):
        return lax.all_to_all(x, "kvp", 0, 0, tiled=True)

    cosine, sine = rotation_tables(positions, lax.axis_index("kvp") * own, own, steps)
    columns = (group + 2) * HEAD_SIZE
    parts = pl.pallas_call(
        project_kernel,
        out_shape=jax.ShapeDtypeStruct((owners, rows, columns), bf16),
        in_specs=[HBM] * 4,
        out_specs=VMEM,
        scratch_shapes=[
            pltpu.VMEM(hidden_in.shape, bf16),
            pltpu.VMEM((hidden_in.shape[2], columns), bf16),
            pltpu.SemaphoreType.DMA((group + 3,)),
        ],
        compiler_params=params(),
    )(hidden_in, w_query, key_weight_matrix, value_weight_matrix)
    parts = exchange(parts)
    queries, new_rows = pl.pallas_call(
        rotate_kernel,
        out_shape=(
            jax.ShapeDtypeStruct((owners, flat, HEAD_SIZE), bf16),
            jax.ShapeDtypeStruct((2, rows, HEAD_SIZE), bf16),
        ),
        in_specs=[VMEM] * 3,
        out_specs=(VMEM, VMEM),
        scratch_shapes=[pltpu.VMEM((flat, HEAD_SIZE), f32)],
        compiler_params=params(),
    )(parts, cosine, sine)
    own_queries = queries[0]
    queries = exchange(queries).reshape(requests, steps * group, HEAD_SIZE)

    batch = 16
    sums = (requests, steps * group, HEAD_SIZE)
    parts = pl.pallas_call(
        functools.partial(attention_kernel, scaling, batch),
        out_shape=jax.ShapeDtypeStruct((owners, flat + STAT_ROWS, HEAD_SIZE), bf16),
        in_specs=[SMEM, SMEM, VMEM, HBM, HBM],
        out_specs=VMEM,
        scratch_shapes=[pltpu.VMEM(paged_key_cache.shape, bf16)] * 2
        + [pltpu.VMEM(sums, f32)] * 3
        + [pltpu.SemaphoreType.DMA((2, blocks // batch))],
        compiler_params=params(32),
    )(block_request, block_fill, queries, paged_key_cache, paged_value_cache)
    parts = exchange(parts)
    heads = pl.pallas_call(
        functools.partial(finish_kernel, scaling),
        out_shape=jax.ShapeDtypeStruct((owners, rows, group * HEAD_SIZE), bf16),
        in_specs=[VMEM] * 3,
        out_specs=VMEM,
        scratch_shapes=[pltpu.VMEM((flat, HEAD_SIZE), f32)],
        compiler_params=params(),
    )(parts, own_queries, new_rows)
    heads = exchange(heads)

    tp = lax.axis_index("tp")
    core = tp % 2
    half = (owners * own, out_columns)
    keep, send = pl.pallas_call(
        output_kernel,
        out_shape=(jax.ShapeDtypeStruct(half, f32), jax.ShapeDtypeStruct(half, bf16)),
        in_specs=[SMEM, VMEM, VMEM],
        out_specs=(VMEM, VMEM),
        compiler_params=params(),
    )(core.reshape(1), heads, w_out)

    devices = lax.axis_size("tp")

    def swap(x, bits):
        return lax.ppermute(x, "tp", [(i, i ^ bits) for i in range(devices)])

    mine = (keep + swap(send, 1).astype(f32)).astype(bf16)
    others = [swap(mine, bits) for bits in (2, 6, 4)]
    near, across, far = (x.astype(f32) for x in others)
    mine = ((mine.astype(f32) + near) + (across + far)).astype(bf16)
    other = swap(mine, 1)
    return jnp.where(core == 0, jnp.stack([mine, other]), jnp.stack([other, mine]))


def solution(mesh):
    return jax.shard_map(
        local,
        mesh=mesh,
        in_specs=(
            P(None, None, "kvp"),
            P("kvp", "tp"),
            P("kvp", "tp"),
            P("kvp", "tp"),
            P("tp", "kvp"),
            P("kvp", None, "tp"),
            P("kvp", None, "tp"),
            P("kvp"),
            P("kvp"),
            P(),
        ),
        out_specs=P(None, None, "kvp"),
        check_vma=False,
    )
```

```python
import functools

import jax
import jax.numpy as jnp
from jax import lax
from jax.experimental import pallas as pl
from jax.experimental.pallas import tpu as pltpu
from jax.sharding import PartitionSpec as P

HEAD_SIZE = 128
STAT_ROWS = 16
PIECES = 3

floor_score = -1e30
rope_base = 500000.0
VMEM = pl.BlockSpec(memory_space=pltpu.VMEM)
SMEM = pl.BlockSpec(memory_space=pltpu.SMEM)
HBM = pl.BlockSpec(memory_space=pltpu.HBM)
NT = (((1,), (1,)), ((), ()))


def params(mib=24):
    return pltpu.CompilerParams(vmem_limit_bytes=mib * 1024 * 1024)


def in_hbm(*arrays):
    return [pltpu.with_memory_space_constraint(a, pltpu.HBM) for a in arrays]


def rotation_tables(positions, first, count, steps):
    half = HEAD_SIZE // 2
    inverse = rope_base ** (-(jnp.arange(half, dtype=jnp.float32) * 2.0 / HEAD_SIZE))
    own = lax.dynamic_slice_in_dim(positions, first, count)
    slots = own[None, :] + jnp.arange(steps, dtype=jnp.int32)[:, None]
    angles = slots.reshape(-1).astype(jnp.float32)[:, None] * inverse
    cosine, sine = jnp.cos(angles), jnp.sin(angles)
    return (
        jnp.concatenate([cosine, cosine], axis=-1),
        jnp.concatenate([-sine, sine], axis=-1),
    )


def project_kernel(hidden_hbm, wq_hbm, wk_hbm, wv_hbm, out_ref, hidden_ref, w_ref, sems):
    steps, requests, width = hidden_ref.shape
    owners, rows, columns = out_ref.shape
    own = rows // steps
    copies = [pltpu.make_async_copy(hidden_hbm, hidden_ref, sems.at[0])]
    chunks = []
    column = 0
    for hbm in (wq_hbm, wk_hbm, wv_hbm):
        total = hbm.shape[1]
        chunk = min(total, 256)
        for start in range(0, total, chunk):
            lanes = slice(column, column + chunk)
            copies.append(
                pltpu.make_async_copy(
                    hbm.at[:, start : start + chunk], w_ref.at[:, lanes], sems.at[len(copies)]
                )
            )
            chunks.append(lanes)
            column += chunk
    for copy in copies:
        copy.start()
    copies[0].wait()
    hidden = hidden_ref[...].reshape(steps * requests, width)
    for copy, lanes in zip(copies[1:], chunks):
        copy.wait()
        part = jnp.dot(hidden, w_ref[:, lanes], preferred_element_type=jnp.float32)
        split = [
            part[s * requests : (s + 1) * requests].reshape(owners, own, -1) for s in range(steps)
        ]
        out_ref[:, :, lanes] = jnp.concatenate(split, axis=1).astype(jnp.bfloat16)


def rotate_kernel(parts_ref, cos_ref, sin_ref, q_ref, new_ref, turned_ref):
    sources, rows, columns = parts_ref.shape
    steps = 2
    own = rows // steps
    group = columns // HEAD_SIZE - 2
    cosine, sine = cos_ref[...], sin_ref[...]

    def head(index):
        lanes = slice(index * HEAD_SIZE, (index + 1) * HEAD_SIZE)
        return jnp.sum(parts_ref[:, :, lanes].astype(jnp.float32), axis=0)

    def rope(x):
        return x * cosine + pltpu.roll(x, HEAD_SIZE // 2, 1) * sine

    for g in range(group):
        x = rope(head(g))
        for s in range(steps):
            turned_ref[pl.ds(s * group + g, own, stride=steps * group), :] = x[
                s * own : (s + 1) * own
            ]
    new_ref[0] = rope(head(group)).astype(jnp.bfloat16)
    new_ref[1] = head(group + 1).astype(jnp.bfloat16)
    queries = turned_ref[...].astype(jnp.bfloat16)
    for d in range(q_ref.shape[0]):
        q_ref[d] = queries


def pieces(x):
    out = []
    for _ in range(PIECES):
        part = x.astype(jnp.bfloat16).astype(jnp.float32)
        out.append(part)
        x = x - part
    return out


def attention_kernel(
    scaling,
    batch,
    request_ref,
    fill_ref,
    q_ref,
    k_hbm,
    v_hbm,
    out_ref,
    k_ref,
    v_ref,
    max_ref,
    total_ref,
    sum_ref,
    sems,
):
    blocks, slots, _ = k_ref.shape
    requests, rows, _ = q_ref.shape
    groups = blocks // batch
    lanes = batch * rows

    def load(hbm, ref, which, g):
        span = pl.ds(g * batch, batch)
        return pltpu.make_async_copy(hbm.at[span], ref.at[span], sems.at[which, g])

    for g in range(groups):
        load(k_hbm, k_ref, 0, g).start()
        load(v_hbm, v_ref, 1, g).start()
    max_ref[...] = jnp.full_like(max_ref, floor_score)
    total_ref[...] = jnp.zeros_like(total_ref)
    sum_ref[...] = jnp.zeros_like(sum_ref)

    slot = lax.broadcasted_iota(jnp.int32, (slots, lanes), 0)
    lane_block = lax.broadcasted_iota(jnp.int32, (1, lanes), 1) // rows
    empty = jnp.zeros((rows, HEAD_SIZE), jnp.bfloat16)

    def group_step(g, _):
        first = g * batch
        owners = [request_ref[first + b] for b in range(batch)]

        def placed(b):
            return jnp.concatenate(
                [empty] * b + [q_ref[owners[b]]] + [empty] * (batch - b - 1), axis=0
            )

        load(k_hbm, k_ref, 0, g).wait()
        scores = jnp.zeros((slots, lanes), jnp.float32)
        for b in range(0, batch, 2):
            scores = scores + lax.dot_general(
                jnp.concatenate([k_ref[first + b], k_ref[first + b + 1]], axis=1),
                jnp.concatenate([placed(b), placed(b + 1)], axis=1),
                NT,
                preferred_element_type=jnp.float32,
            )
        fill = jnp.zeros((1, lanes), jnp.int32)
        for b in range(batch):
            fill = jnp.where(lane_block == b, fill_ref[first + b], fill)
        scores = jnp.where(slot < fill, scores * scaling, floor_score)
        largest = jnp.max(scores, axis=0, keepdims=True)
        weights = jnp.exp(scores - largest).astype(jnp.bfloat16).astype(jnp.float32)
        total = jnp.sum(weights, axis=0, keepdims=True)
        turned = weights.T.astype(jnp.bfloat16)
        stats = jnp.concatenate(
            [largest, total, jnp.zeros((6, lanes), jnp.float32)], axis=0
        ).T
        load(v_hbm, v_ref, 1, g).wait()
        for b in range(batch):
            mine = slice(b * rows, (b + 1) * rows)
            summed = jnp.dot(turned[mine], v_ref[first + b], preferred_element_type=jnp.float32)
            owner = owners[b]
            before = max_ref[owner]
            block_max = stats[mine, 0:1]
            after = jnp.maximum(before, block_max)
            keep = jnp.exp(before - after)
            add = jnp.exp(block_max - after)
            max_ref[owner] = after
            total_ref[owner] = total_ref[owner] * keep + stats[mine, 1:2] * add
            sum_ref[owner] = sum_ref[owner] * keep + summed * add
        return 0

    lax.fori_loop(0, groups, group_step, 0)

    owners = out_ref.shape[0]
    own = requests // owners
    flat = own * rows
    lane = lax.broadcasted_iota(jnp.int32, (flat, HEAD_SIZE), 1)
    pick = (
        lax.broadcasted_iota(jnp.int32, (STAT_ROWS, HEAD_SIZE), 0)
        == lax.broadcasted_iota(jnp.int32, (STAT_ROWS, HEAD_SIZE), 1)
    ).astype(jnp.bfloat16)
    for d in range(owners):
        mine = slice(d * own, (d + 1) * own)
        out_ref[d, :flat, :] = sum_ref[mine].reshape(flat, HEAD_SIZE).astype(jnp.bfloat16)
        values = pieces(max_ref[mine].reshape(flat, HEAD_SIZE)) + pieces(
            total_ref[mine].reshape(flat, HEAD_SIZE)
        )
        table = jnp.zeros((flat, HEAD_SIZE), jnp.float32)
        for i, value in enumerate(values):
            table = jnp.where(lane == i, value, table)
        out_ref[d, flat:, :] = lax.dot_general(
            pick, table.astype(jnp.bfloat16), NT, preferred_element_type=jnp.float32
        ).astype(jnp.bfloat16)


def finish_kernel(scaling, parts_ref, q_ref, new_ref, out_ref, heads_ref):
    sources = parts_ref.shape[0]
    flat = q_ref.shape[0]
    steps = 2
    own = new_ref.shape[1] // steps
    rows = flat // own
    group = rows // steps

    stats = parts_ref[:, flat:, :].astype(jnp.float32)
    largest = sum(stats[:, i, :] for i in range(PIECES))
    total = sum(stats[:, PIECES + i, :] for i in range(PIECES))
    pad = HEAD_SIZE - sources
    largest = jnp.concatenate([largest, jnp.full((pad, flat), floor_score, jnp.float32)], axis=0).T
    total = jnp.concatenate([total, jnp.zeros((pad, flat), jnp.float32)], axis=0).T

    def spread(x):
        return jnp.broadcast_to(x[:, None, :], (own, rows, HEAD_SIZE)).reshape(flat, HEAD_SIZE)

    queries = q_ref[...].astype(jnp.float32)
    keys = new_ref[0].astype(jnp.float32)
    values = new_ref[1].astype(jnp.float32)
    row = lax.broadcasted_iota(jnp.int32, (flat, 1), 0)
    row_step = (row % rows) // group
    scores = []
    for t in range(steps):
        score = (
            jnp.sum(queries * spread(keys[t * own : (t + 1) * own]), axis=1, keepdims=True)
            * scaling
        )
        scores.append(jnp.where(row_step >= t, score, floor_score))
    peak = jnp.max(largest, axis=1, keepdims=True)
    for score in scores:
        peak = jnp.maximum(peak, score)
    factor = jnp.exp(largest - peak)
    weight_total = jnp.sum(factor * total, axis=1, keepdims=True)
    summed = jnp.zeros((flat, HEAD_SIZE), jnp.float32)
    for source in range(sources):
        summed = summed + factor[:, source : source + 1] * parts_ref[source, :flat, :].astype(
            jnp.float32
        )
    for t in range(steps):
        weight = jnp.exp(scores[t] - peak).astype(jnp.bfloat16).astype(jnp.float32)
        weight_total = weight_total + weight
        summed = summed + weight * spread(values[t * own : (t + 1) * own])
    heads_ref[...] = summed / weight_total
    columns = []
    for g in range(group):
        columns.append(
            jnp.concatenate(
                [
                    heads_ref[pl.ds(s * group + g, own, stride=rows), :]
                    for s in range(steps)
                ],
                axis=0,
            )
        )
    heads = jnp.concatenate(columns, axis=1).astype(jnp.bfloat16)
    for d in range(out_ref.shape[0]):
        out_ref[d] = heads


def output_kernel(core_ref, heads_ref, w_ref, keep_ref, send_ref):
    owners, rows, width = heads_ref.shape
    steps = 2
    own = rows // steps
    core = core_ref[0]
    heads = heads_ref[...].reshape(owners * rows, width)
    columns = w_ref.shape[1]
    chunk = min(columns, 256)
    for start in range(0, columns, chunk):
        lanes = slice(start, start + chunk)
        part = jnp.dot(heads, w_ref[:, lanes], preferred_element_type=jnp.float32)
        part = part.reshape(owners, rows, chunk)
        first = part[:, :own].reshape(owners * own, chunk)
        second = part[:, own:].reshape(owners * own, chunk)
        keep_ref[:, lanes] = jnp.where(core == 0, first, second)
        send_ref[:, lanes] = jnp.where(core == 0, second, first).astype(jnp.bfloat16)


def local(
    hidden_in,
    w_query,
    key_weight_matrix,
    value_weight_matrix,
    w_out,
    paged_key_cache,
    paged_value_cache,
    block_request,
    block_fill,
    positions,
):
    bf16, f32 = jnp.bfloat16, jnp.float32
    steps, requests, _ = hidden_in.shape
    group = w_query.shape[1] // HEAD_SIZE
    owners = lax.axis_size("kvp")
    own = requests // owners
    rows = steps * own
    flat = rows * group
    scaling = HEAD_SIZE ** (-0.5)
    blocks, slots, _ = paged_key_cache.shape
    out_columns = w_out.shape[1]

    def exchange(x):
        return lax.all_to_all(x, "kvp", 0, 0, tiled=True)

    cosine, sine = rotation_tables(positions, lax.axis_index("kvp") * own, own, steps)
    columns = (group + 2) * HEAD_SIZE
    parts = pl.pallas_call(
        project_kernel,
        out_shape=jax.ShapeDtypeStruct((owners, rows, columns), bf16),
        in_specs=[HBM] * 4,
        out_specs=VMEM,
        scratch_shapes=[
            pltpu.VMEM(hidden_in.shape, bf16),
            pltpu.VMEM((hidden_in.shape[2], columns), bf16),
            pltpu.SemaphoreType.DMA((group + 3,)),
        ],
        compiler_params=params(),
    )(*in_hbm(hidden_in, w_query, key_weight_matrix, value_weight_matrix))
    parts = exchange(parts)
    queries, new_rows = pl.pallas_call(
        rotate_kernel,
        out_shape=(
            jax.ShapeDtypeStruct((owners, flat, HEAD_SIZE), bf16),
            jax.ShapeDtypeStruct((2, rows, HEAD_SIZE), bf16),
        ),
        in_specs=[VMEM] * 3,
        out_specs=(VMEM, VMEM),
        scratch_shapes=[pltpu.VMEM((flat, HEAD_SIZE), f32)],
        compiler_params=params(),
    )(parts, cosine, sine)
    own_queries = queries[0]
    queries = exchange(queries).reshape(requests, steps * group, HEAD_SIZE)

    batch = 16
    sums = (requests, steps * group, HEAD_SIZE)
    parts = pl.pallas_call(
        functools.partial(attention_kernel, scaling, batch),
        out_shape=jax.ShapeDtypeStruct((owners, flat + STAT_ROWS, HEAD_SIZE), bf16),
        in_specs=[SMEM, SMEM, VMEM, HBM, HBM],
        out_specs=VMEM,
        scratch_shapes=[pltpu.VMEM(paged_key_cache.shape, bf16)] * 2
        + [pltpu.VMEM(sums, f32)] * 3
        + [pltpu.SemaphoreType.DMA((2, blocks // batch))],
        compiler_params=params(32),
    )(block_request, block_fill, queries, *in_hbm(paged_key_cache, paged_value_cache))
    parts = exchange(parts)
    heads = pl.pallas_call(
        functools.partial(finish_kernel, scaling),
        out_shape=jax.ShapeDtypeStruct((owners, rows, group * HEAD_SIZE), bf16),
        in_specs=[VMEM] * 3,
        out_specs=VMEM,
        scratch_shapes=[pltpu.VMEM((flat, HEAD_SIZE), f32)],
        compiler_params=params(),
    )(parts, own_queries, new_rows)
    heads = exchange(heads)

    tp = lax.axis_index("tp")
    core = tp % 2
    half = (owners * own, out_columns)
    keep, send = pl.pallas_call(
        output_kernel,
        out_shape=(jax.ShapeDtypeStruct(half, f32), jax.ShapeDtypeStruct(half, bf16)),
        in_specs=[SMEM, VMEM, VMEM],
        out_specs=(VMEM, VMEM),
        compiler_params=params(),
    )(core.reshape(1), heads, w_out)

    devices = lax.axis_size("tp")

    def swap(x, bits):
        return lax.ppermute(x, "tp", [(i, i ^ bits) for i in range(devices)])

    mine = (keep + swap(send, 1).astype(f32)).astype(bf16)
    others = [swap(mine, bits) for bits in (2, 6, 4)]
    near, across, far = (x.astype(f32) for x in others)
    mine = ((mine.astype(f32) + near) + (across + far)).astype(bf16)
    other = swap(mine, 1)
    return jnp.where(core == 0, jnp.stack([mine, other]), jnp.stack([other, mine]))


def solution(mesh):
    return jax.shard_map(
        local,
        mesh=mesh,
        in_specs=(
            P(None, None, "kvp"),
            P("kvp", "tp"),
            P("kvp", "tp"),
            P("kvp", "tp"),
            P("tp", "kvp"),
            P("kvp", None, "tp"),
            P("kvp", None, "tp"),
            P("kvp"),
            P("kvp"),
            P(),
        ),
        out_specs=P(None, None, "kvp"),
        check_vma=False,
    )
```

```python
import functools

import jax
import jax.numpy as jnp
from jax import lax
from jax.experimental import pallas as pl
from jax.experimental.pallas import tpu as pltpu
from jax.sharding import PartitionSpec as P

HEAD_SIZE = 128
STAT_ROWS = 16
PIECES = 3

floor_score = -1e30
rope_base = 500000.0
VMEM = pl.BlockSpec(memory_space=pltpu.VMEM)
SMEM = pl.BlockSpec(memory_space=pltpu.SMEM)
HBM = pl.BlockSpec(memory_space=pltpu.HBM)
NT = (((1,), (1,)), ((), ()))


def params(mib=24):
    return pltpu.CompilerParams(vmem_limit_bytes=mib * 1024 * 1024)


def in_hbm(*arrays):
    return [pltpu.with_memory_space_constraint(a, pltpu.HBM) for a in arrays]


def rotation_tables(slots):
    half = HEAD_SIZE // 2
    inverse = rope_base ** (-(jnp.arange(half, dtype=jnp.float32) * 2.0 / HEAD_SIZE))
    angles = slots[:, :half] * inverse
    cosine, sine = jnp.cos(angles), jnp.sin(angles)
    return (
        jnp.concatenate([cosine, cosine], axis=-1),
        jnp.concatenate([-sine, sine], axis=-1),
    )


def project_kernel(
    position_hbm,
    hidden_hbm,
    wq_hbm,
    wk_hbm,
    wv_hbm,
    out_ref,
    slot_ref,
    position_ref,
    hidden_ref,
    wq_ref,
    wk_ref,
    wv_ref,
    sems,
):
    steps, requests, width = hidden_ref.shape
    owners, rows, columns = out_ref.shape
    own = rows // steps
    sources = (position_hbm, hidden_hbm, wk_hbm, wv_hbm, wq_hbm)
    targets = (position_ref, hidden_ref, wk_ref, wv_ref, wq_ref)
    copies = [
        pltpu.make_async_copy(source, target, sems.at[i])
        for i, (source, target) in enumerate(zip(sources, targets))
    ]
    for copy in copies:
        copy.start()
    first = lax.axis_index("kvp") * own
    copies[0].wait()
    row = lax.broadcasted_iota(jnp.int32, (rows, HEAD_SIZE), 0)
    slots = jnp.zeros((rows, HEAD_SIZE), jnp.int32)
    for r in range(own):
        slots = jnp.where(row % own == r, position_ref[first + r], slots)
    slot_ref[...] = (slots + row // own).astype(jnp.float32)
    copies[1].wait()
    hidden = hidden_ref[...].reshape(steps * requests, width)
    queries = wq_ref.shape[1]
    starts = (queries, queries + wk_ref.shape[1], 0)
    for copy, ref, column in zip(copies[2:], targets[2:], starts):
        copy.wait()
        total = ref.shape[1]
        chunk = min(total, 256)
        for start in range(0, total, chunk):
            part = jnp.dot(
                hidden, ref[:, start : start + chunk], preferred_element_type=jnp.float32
            )
            split = [
                part[s * requests : (s + 1) * requests].reshape(owners, own, chunk)
                for s in range(steps)
            ]
            lanes = slice(column + start, column + start + chunk)
            out_ref[:, :, lanes] = jnp.concatenate(split, axis=1).astype(jnp.bfloat16)


def rotate_kernel(parts_ref, cos_ref, sin_ref, q_ref, own_ref, new_ref, turned_ref):
    sources, rows, columns = parts_ref.shape
    steps = 2
    own = rows // steps
    group = columns // HEAD_SIZE - 2
    cosine, sine = cos_ref[...], sin_ref[...]

    def head(index):
        lanes = slice(index * HEAD_SIZE, (index + 1) * HEAD_SIZE)
        return jnp.sum(parts_ref[:, :, lanes].astype(jnp.float32), axis=0)

    def rope(x):
        return x * cosine + pltpu.roll(x, HEAD_SIZE // 2, 1) * sine

    for g in range(group):
        x = rope(head(g))
        for s in range(steps):
            turned_ref[pl.ds(s * group + g, own, stride=steps * group), :] = x[
                s * own : (s + 1) * own
            ]
    new_ref[0] = rope(head(group)).astype(jnp.bfloat16)
    new_ref[1] = head(group + 1).astype(jnp.bfloat16)
    queries = turned_ref[...].astype(jnp.bfloat16)
    own_ref[...] = queries
    for d in range(q_ref.shape[0]):
        q_ref[d] = queries


def pieces(x):
    out = []
    for _ in range(PIECES):
        part = x.astype(jnp.bfloat16).astype(jnp.float32)
        out.append(part)
        x = x - part
    return out


def attention_kernel(
    scaling,
    batch,
    request_ref,
    fill_ref,
    q_ref,
    k_hbm,
    v_hbm,
    out_ref,
    k_ref,
    v_ref,
    max_ref,
    total_ref,
    sum_ref,
    sems,
):
    blocks, slots, _ = k_ref.shape
    requests, rows, _ = q_ref.shape
    groups = blocks // batch
    lanes = batch * rows

    def load(hbm, ref, which, g):
        span = pl.ds(g * batch, batch)
        return pltpu.make_async_copy(hbm.at[span], ref.at[span], sems.at[which, g])

    for g in range(groups):
        load(k_hbm, k_ref, 0, g).start()
        load(v_hbm, v_ref, 1, g).start()
    max_ref[...] = jnp.full_like(max_ref, floor_score)
    total_ref[...] = jnp.zeros_like(total_ref)
    sum_ref[...] = jnp.zeros_like(sum_ref)

    slot = lax.broadcasted_iota(jnp.int32, (lanes, slots), 1)

    def score(g):
        first = g * batch
        load(k_hbm, k_ref, 0, g).wait()
        return jnp.concatenate(
            [
                lax.dot_general(
                    q_ref[request_ref[first + b]],
                    k_ref[first + b],
                    NT,
                    preferred_element_type=jnp.float32,
                )
                for b in range(batch)
            ],
            axis=0,
        )

    def weigh(g, scores):
        first = g * batch
        fill = jnp.concatenate(
            [jnp.full((rows, 1), fill_ref[first + b], jnp.int32) for b in range(batch)], axis=0
        )
        scores = jnp.where(slot < fill, scores * scaling, floor_score)
        largest = jnp.max(scores, axis=1, keepdims=True)
        weights = jnp.exp(scores - largest).astype(jnp.bfloat16)
        total = jnp.sum(weights.astype(jnp.float32), axis=1, keepdims=True)
        load(v_hbm, v_ref, 1, g).wait()
        summed = [
            jnp.dot(
                weights[b * rows : (b + 1) * rows],
                v_ref[first + b],
                preferred_element_type=jnp.float32,
            )
            for b in range(batch)
        ]
        return largest, total, summed

    def merge(g, largest, total, summed):
        for b in range(batch):
            mine = slice(b * rows, (b + 1) * rows)
            owner = request_ref[g * batch + b]
            before = max_ref[owner]
            after = jnp.maximum(before, largest[mine])
            keep = jnp.exp(before - after)
            add = jnp.exp(largest[mine] - after)
            max_ref[owner] = after
            total_ref[owner] = total_ref[owner] * keep + total[mine] * add
            sum_ref[owner] = sum_ref[owner] * keep + summed[b] * add

    scores = score(0)
    for g in range(groups):
        later = score(g + 1) if g + 1 < groups else None
        merge(g, *weigh(g, scores))
        scores = later

    owners = out_ref.shape[0]
    own = requests // owners
    flat = own * rows
    diagonal = lax.broadcasted_iota(jnp.int32, (flat, HEAD_SIZE), 0) == lax.broadcasted_iota(
        jnp.int32, (flat, HEAD_SIZE), 1
    )

    def by_lane(ref):
        return jnp.concatenate(
            [
                jnp.sum(
                    jnp.where(
                        diagonal, ref[d * own : (d + 1) * own].reshape(flat, HEAD_SIZE), 0.0
                    ),
                    axis=0,
                    keepdims=True,
                )
                for d in range(owners)
            ],
            axis=0,
        )

    values = pieces(by_lane(max_ref)) + pieces(by_lane(total_ref))
    empty = jnp.zeros((STAT_ROWS - len(values), HEAD_SIZE), jnp.float32)
    for d in range(owners):
        out_ref[d, :flat, :] = (
            sum_ref[d * own : (d + 1) * own].reshape(flat, HEAD_SIZE).astype(jnp.bfloat16)
        )
        out_ref[d, flat:, :] = jnp.concatenate(
            [value[d : d + 1] for value in values] + [empty], axis=0
        ).astype(jnp.bfloat16)


def finish_kernel(scaling, parts_ref, q_ref, new_ref, out_ref, heads_ref):
    sources = parts_ref.shape[0]
    flat = q_ref.shape[0]
    steps = 2
    own = new_ref.shape[1] // steps
    rows = flat // own
    group = rows // steps

    stats = parts_ref[:, flat:, :].astype(jnp.float32)
    largest = sum(stats[:, i, :] for i in range(PIECES))
    total = sum(stats[:, PIECES + i, :] for i in range(PIECES))
    pad = HEAD_SIZE - sources
    largest = jnp.concatenate([largest, jnp.full((pad, flat), floor_score, jnp.float32)], axis=0).T
    total = jnp.concatenate([total, jnp.zeros((pad, flat), jnp.float32)], axis=0).T

    def spread(x):
        return jnp.broadcast_to(x[:, None, :], (own, rows, HEAD_SIZE)).reshape(flat, HEAD_SIZE)

    queries = q_ref[...].astype(jnp.float32)
    keys = new_ref[0].astype(jnp.float32)
    values = new_ref[1].astype(jnp.float32)
    row = lax.broadcasted_iota(jnp.int32, (flat, 1), 0)
    row_step = (row % rows) // group
    scores = []
    for t in range(steps):
        score = (
            jnp.sum(queries * spread(keys[t * own : (t + 1) * own]), axis=1, keepdims=True)
            * scaling
        )
        scores.append(jnp.where(row_step >= t, score, floor_score))
    peak = jnp.max(largest, axis=1, keepdims=True)
    for score in scores:
        peak = jnp.maximum(peak, score)
    factor = jnp.exp(largest - peak)
    weight_total = jnp.sum(factor * total, axis=1, keepdims=True)
    summed = jnp.zeros((flat, HEAD_SIZE), jnp.float32)
    for source in range(sources):
        summed = summed + factor[:, source : source + 1] * parts_ref[source, :flat, :].astype(
            jnp.float32
        )
    for t in range(steps):
        weight = jnp.exp(scores[t] - peak).astype(jnp.bfloat16).astype(jnp.float32)
        weight_total = weight_total + weight
        summed = summed + weight * spread(values[t * own : (t + 1) * own])
    heads_ref[...] = summed / weight_total
    columns = []
    for g in range(group):
        columns.append(
            jnp.concatenate(
                [
                    heads_ref[pl.ds(s * group + g, own, stride=rows), :]
                    for s in range(steps)
                ],
                axis=0,
            )
        )
    heads = jnp.concatenate(columns, axis=1).astype(jnp.bfloat16)
    for d in range(out_ref.shape[0]):
        out_ref[d] = heads


def output_kernel(core_ref, heads_ref, w_ref, keep_ref, send_ref):
    owners, rows, width = heads_ref.shape
    steps = 2
    own = rows // steps
    core = core_ref[0]
    heads = heads_ref[...].reshape(owners * rows, width)
    columns = w_ref.shape[1]
    chunk = min(columns, 256)
    for start in range(0, columns, chunk):
        lanes = slice(start, start + chunk)
        part = jnp.dot(heads, w_ref[:, lanes], preferred_element_type=jnp.float32)
        part = part.reshape(owners, rows, chunk)
        first = part[:, :own].reshape(owners * own, chunk)
        second = part[:, own:].reshape(owners * own, chunk)
        keep_ref[:, lanes] = jnp.where(core == 0, first, second)
        send_ref[:, lanes] = jnp.where(core == 0, second, first).astype(jnp.bfloat16)


def local(
    hidden_in,
    w_query,
    key_weight_matrix,
    value_weight_matrix,
    w_out,
    paged_key_cache,
    paged_value_cache,
    block_request,
    block_fill,
    positions,
):
    bf16, f32 = jnp.bfloat16, jnp.float32
    steps, requests, _ = hidden_in.shape
    group = w_query.shape[1] // HEAD_SIZE
    owners = lax.axis_size("kvp")
    own = requests // owners
    rows = steps * own
    flat = rows * group
    scaling = HEAD_SIZE ** (-0.5)
    blocks, slots, _ = paged_key_cache.shape
    out_columns = w_out.shape[1]

    def exchange(x):
        return lax.all_to_all(x, "kvp", 0, 0, tiled=True)

    tp = lax.axis_index("tp")
    core = tp % 2
    hidden_in, core = lax.optimization_barrier((hidden_in, core))
    columns = (group + 2) * HEAD_SIZE
    parts, row_slots = pl.pallas_call(
        project_kernel,
        out_shape=(
            jax.ShapeDtypeStruct((owners, rows, columns), bf16),
            jax.ShapeDtypeStruct((rows, HEAD_SIZE), f32),
        ),
        in_specs=[HBM] * 5,
        out_specs=(VMEM, VMEM),
        scratch_shapes=[
            pltpu.SMEM(positions.shape, jnp.int32),
            pltpu.VMEM(hidden_in.shape, bf16),
            pltpu.VMEM(w_query.shape, bf16),
            pltpu.VMEM(key_weight_matrix.shape, bf16),
            pltpu.VMEM(value_weight_matrix.shape, bf16),
            pltpu.SemaphoreType.DMA((5,)),
        ],
        compiler_params=params(),
    )(*in_hbm(positions, hidden_in, w_query, key_weight_matrix, value_weight_matrix))
    cosine, sine = rotation_tables(row_slots)
    parts, cosine, sine = lax.optimization_barrier((parts, cosine, sine))
    parts = exchange(parts)
    queries, own_queries, new_rows = pl.pallas_call(
        rotate_kernel,
        out_shape=(
            jax.ShapeDtypeStruct((owners, flat, HEAD_SIZE), bf16),
            jax.ShapeDtypeStruct((flat, HEAD_SIZE), bf16),
            jax.ShapeDtypeStruct((2, rows, HEAD_SIZE), bf16),
        ),
        in_specs=[VMEM] * 3,
        out_specs=(VMEM, VMEM, VMEM),
        scratch_shapes=[pltpu.VMEM((flat, HEAD_SIZE), f32)],
        compiler_params=params(),
    )(parts, cosine, sine)
    queries = exchange(queries).reshape(requests, steps * group, HEAD_SIZE)

    batch = 16
    sums = (requests, steps * group, HEAD_SIZE)
    parts = pl.pallas_call(
        functools.partial(attention_kernel, scaling, batch),
        out_shape=jax.ShapeDtypeStruct((owners, flat + STAT_ROWS, HEAD_SIZE), bf16),
        in_specs=[SMEM, SMEM, VMEM, HBM, HBM],
        out_specs=VMEM,
        scratch_shapes=[pltpu.VMEM(paged_key_cache.shape, bf16)] * 2
        + [pltpu.VMEM(sums, f32)] * 3
        + [pltpu.SemaphoreType.DMA((2, blocks // batch))],
        compiler_params=params(32),
    )(block_request, block_fill, queries, *in_hbm(paged_key_cache, paged_value_cache))
    parts = exchange(parts)
    heads = pl.pallas_call(
        functools.partial(finish_kernel, scaling),
        out_shape=jax.ShapeDtypeStruct((owners, rows, group * HEAD_SIZE), bf16),
        in_specs=[VMEM] * 3,
        out_specs=VMEM,
        scratch_shapes=[pltpu.VMEM((flat, HEAD_SIZE), f32)],
        compiler_params=params(),
    )(parts, own_queries, new_rows)
    heads = exchange(heads)

    half = (owners * own, out_columns)
    keep, send = pl.pallas_call(
        output_kernel,
        out_shape=(jax.ShapeDtypeStruct(half, f32), jax.ShapeDtypeStruct(half, bf16)),
        in_specs=[SMEM, VMEM, VMEM],
        out_specs=(VMEM, VMEM),
        compiler_params=params(),
    )(core.reshape(1), heads, w_out)

    devices = lax.axis_size("tp")

    def swap(x, bits):
        return lax.ppermute(x, "tp", [(i, i ^ bits) for i in range(devices)])

    mine = (keep + swap(send, 1).astype(f32)).astype(bf16)
    others = [swap(mine, bits) for bits in (2, 6, 4)]
    near, across, far = (x.astype(f32) for x in others)
    mine = ((mine.astype(f32) + near) + (across + far)).astype(bf16)
    other = swap(mine, 1)
    return jnp.where(core == 0, jnp.stack([mine, other]), jnp.stack([other, mine]))


def solution(mesh):
    return jax.shard_map(
        local,
        mesh=mesh,
        in_specs=(
            P(None, None, "kvp"),
            P("kvp", "tp"),
            P("kvp", "tp"),
            P("kvp", "tp"),
            P("tp", "kvp"),
            P("kvp", None, "tp"),
            P("kvp", None, "tp"),
            P("kvp"),
            P("kvp"),
            P(),
        ),
        out_specs=P(None, None, "kvp"),
        check_vma=False,
    )
```

```python
import functools

import jax
import jax.numpy as jnp
from jax import lax
from jax.experimental import pallas as pl
from jax.experimental.pallas import tpu as pltpu
from jax.sharding import PartitionSpec as P

HEAD_SIZE = 128
STAT_ROWS = 16
PIECES = 3

floor_score = -1e30
rope_base = 500000.0
VMEM = pl.BlockSpec(memory_space=pltpu.VMEM)
SMEM = pl.BlockSpec(memory_space=pltpu.SMEM)
HBM = pl.BlockSpec(memory_space=pltpu.HBM)
NT = (((1,), (1,)), ((), ()))


def params(mib=24):
    return pltpu.CompilerParams(vmem_limit_bytes=mib * 1024 * 1024)


def in_hbm(*arrays):
    return [pltpu.with_memory_space_constraint(a, pltpu.HBM) for a in arrays]


def in_vmem(*arrays):
    return [pltpu.with_memory_space_constraint(a, pltpu.VMEM) for a in arrays]


def rotation_tables(slots):
    half = HEAD_SIZE // 2
    inverse = rope_base ** (-(jnp.arange(half, dtype=jnp.float32) * 2.0 / HEAD_SIZE))
    angles = slots[:, :half] * inverse
    cosine, sine = jnp.cos(angles), jnp.sin(angles)
    return (
        jnp.concatenate([cosine, cosine], axis=-1),
        jnp.concatenate([-sine, sine], axis=-1),
    )


def project_kernel(
    position_hbm,
    hidden_hbm,
    wq_hbm,
    wk_hbm,
    wv_hbm,
    out_ref,
    slot_ref,
    position_ref,
    hidden_ref,
    wq_ref,
    wk_ref,
    wv_ref,
    sems,
):
    steps, requests, width = hidden_ref.shape
    owners, rows, columns = out_ref.shape
    own = rows // steps
    sources = (position_hbm, hidden_hbm, wk_hbm, wv_hbm, wq_hbm)
    targets = (position_ref, hidden_ref, wk_ref, wv_ref, wq_ref)
    copies = [
        pltpu.make_async_copy(source, target, sems.at[i])
        for i, (source, target) in enumerate(zip(sources, targets))
    ]
    for copy in copies:
        copy.start()
    first = lax.axis_index("kvp") * own
    copies[0].wait()
    row = lax.broadcasted_iota(jnp.int32, (rows, HEAD_SIZE), 0)
    slots = jnp.zeros((rows, HEAD_SIZE), jnp.int32)
    for r in range(own):
        slots = jnp.where(row % own == r, position_ref[first + r], slots)
    slot_ref[...] = (slots + row // own).astype(jnp.float32)
    copies[1].wait()
    hidden = hidden_ref[...].reshape(steps * requests, width)
    queries = wq_ref.shape[1]
    starts = (queries, queries + wk_ref.shape[1], 0)
    for copy, ref, column in zip(copies[2:], targets[2:], starts):
        copy.wait()
        total = ref.shape[1]
        chunk = min(total, 256)
        for start in range(0, total, chunk):
            part = jnp.dot(
                hidden, ref[:, start : start + chunk], preferred_element_type=jnp.float32
            )
            split = [
                part[s * requests : (s + 1) * requests].reshape(owners, own, chunk)
                for s in range(steps)
            ]
            lanes = slice(column + start, column + start + chunk)
            out_ref[:, :, lanes] = jnp.concatenate(split, axis=1).astype(jnp.bfloat16)


def rotate_kernel(parts_ref, cos_ref, sin_ref, keys_hbm, values_hbm, q_ref, own_ref, new_ref, turned_ref):
    sources, rows, columns = parts_ref.shape
    steps = 2
    own = rows // steps
    group = columns // HEAD_SIZE - 2
    cosine, sine = cos_ref[...], sin_ref[...]

    def head(index):
        lanes = slice(index * HEAD_SIZE, (index + 1) * HEAD_SIZE)
        return jnp.sum(parts_ref[:, :, lanes].astype(jnp.float32), axis=0)

    def rope(x):
        return x * cosine + pltpu.roll(x, HEAD_SIZE // 2, 1) * sine

    for g in range(group):
        x = rope(head(g))
        for s in range(steps):
            turned_ref[pl.ds(s * group + g, own, stride=steps * group), :] = x[
                s * own : (s + 1) * own
            ]
    new_ref[0] = rope(head(group)).astype(jnp.bfloat16)
    new_ref[1] = head(group + 1).astype(jnp.bfloat16)
    queries = turned_ref[...].astype(jnp.bfloat16)
    own_ref[...] = queries
    for d in range(q_ref.shape[0]):
        q_ref[d] = queries


def pieces(x):
    out = []
    for _ in range(PIECES):
        part = x.astype(jnp.bfloat16).astype(jnp.float32)
        out.append(part)
        x = x - part
    return out


def attention_kernel(
    scaling,
    batch,
    request_ref,
    fill_ref,
    q_ref,
    k_ref,
    v_ref,
    out_ref,
    max_ref,
    total_ref,
    sum_ref,
):
    blocks, slots, _ = k_ref.shape
    requests, rows, _ = q_ref.shape
    groups = blocks // batch
    lanes = batch * rows

    max_ref[...] = jnp.full_like(max_ref, floor_score)
    total_ref[...] = jnp.zeros_like(total_ref)
    sum_ref[...] = jnp.zeros_like(sum_ref)

    slot = lax.broadcasted_iota(jnp.int32, (lanes, slots), 1)

    def score(g):
        first = g * batch
        return jnp.concatenate(
            [
                lax.dot_general(
                    q_ref[request_ref[first + b]],
                    k_ref[first + b],
                    NT,
                    preferred_element_type=jnp.float32,
                )
                for b in range(batch)
            ],
            axis=0,
        )

    def weigh(g, scores):
        first = g * batch
        fill = jnp.concatenate(
            [jnp.full((rows, 1), fill_ref[first + b], jnp.int32) for b in range(batch)], axis=0
        )
        scores = jnp.where(slot < fill, scores * scaling, floor_score)
        largest = jnp.max(scores, axis=1, keepdims=True)
        weights = jnp.exp(scores - largest).astype(jnp.bfloat16)
        total = jnp.sum(weights.astype(jnp.float32), axis=1, keepdims=True)
        summed = [
            jnp.dot(
                weights[b * rows : (b + 1) * rows],
                v_ref[first + b],
                preferred_element_type=jnp.float32,
            )
            for b in range(batch)
        ]
        return largest, total, summed

    def merge(g, largest, total, summed):
        for b in range(batch):
            mine = slice(b * rows, (b + 1) * rows)
            owner = request_ref[g * batch + b]
            before = max_ref[owner]
            after = jnp.maximum(before, largest[mine])
            keep = jnp.exp(before - after)
            add = jnp.exp(largest[mine] - after)
            max_ref[owner] = after
            total_ref[owner] = total_ref[owner] * keep + total[mine] * add
            sum_ref[owner] = sum_ref[owner] * keep + summed[b] * add

    scores = score(0)
    for g in range(groups):
        later = score(g + 1) if g + 1 < groups else None
        merge(g, *weigh(g, scores))
        scores = later

    owners = out_ref.shape[0]
    own = requests // owners
    flat = own * rows
    diagonal = lax.broadcasted_iota(jnp.int32, (flat, HEAD_SIZE), 0) == lax.broadcasted_iota(
        jnp.int32, (flat, HEAD_SIZE), 1
    )

    def by_lane(ref):
        return jnp.concatenate(
            [
                jnp.sum(
                    jnp.where(
                        diagonal, ref[d * own : (d + 1) * own].reshape(flat, HEAD_SIZE), 0.0
                    ),
                    axis=0,
                    keepdims=True,
                )
                for d in range(owners)
            ],
            axis=0,
        )

    values = pieces(by_lane(max_ref)) + pieces(by_lane(total_ref))
    empty = jnp.zeros((STAT_ROWS - len(values), HEAD_SIZE), jnp.float32)
    for d in range(owners):
        out_ref[d, :flat, :] = (
            sum_ref[d * own : (d + 1) * own].reshape(flat, HEAD_SIZE).astype(jnp.bfloat16)
        )
        out_ref[d, flat:, :] = jnp.concatenate(
            [value[d : d + 1] for value in values] + [empty], axis=0
        ).astype(jnp.bfloat16)


def finish_kernel(scaling, parts_ref, q_ref, new_ref, out_ref, heads_ref):
    sources = parts_ref.shape[0]
    flat = q_ref.shape[0]
    steps = 2
    own = new_ref.shape[1] // steps
    rows = flat // own
    group = rows // steps

    stats = parts_ref[:, flat:, :].astype(jnp.float32)
    largest = sum(stats[:, i, :] for i in range(PIECES))
    total = sum(stats[:, PIECES + i, :] for i in range(PIECES))
    pad = HEAD_SIZE - sources
    largest = jnp.concatenate([largest, jnp.full((pad, flat), floor_score, jnp.float32)], axis=0).T
    total = jnp.concatenate([total, jnp.zeros((pad, flat), jnp.float32)], axis=0).T

    def spread(x):
        return jnp.broadcast_to(x[:, None, :], (own, rows, HEAD_SIZE)).reshape(flat, HEAD_SIZE)

    queries = q_ref[...].astype(jnp.float32)
    keys = new_ref[0].astype(jnp.float32)
    values = new_ref[1].astype(jnp.float32)
    row = lax.broadcasted_iota(jnp.int32, (flat, 1), 0)
    row_step = (row % rows) // group
    scores = []
    for t in range(steps):
        score = (
            jnp.sum(queries * spread(keys[t * own : (t + 1) * own]), axis=1, keepdims=True)
            * scaling
        )
        scores.append(jnp.where(row_step >= t, score, floor_score))
    peak = jnp.max(largest, axis=1, keepdims=True)
    for score in scores:
        peak = jnp.maximum(peak, score)
    factor = jnp.exp(largest - peak)
    weight_total = jnp.sum(factor * total, axis=1, keepdims=True)
    summed = jnp.zeros((flat, HEAD_SIZE), jnp.float32)
    for source in range(sources):
        summed = summed + factor[:, source : source + 1] * parts_ref[source, :flat, :].astype(
            jnp.float32
        )
    for t in range(steps):
        weight = jnp.exp(scores[t] - peak).astype(jnp.bfloat16).astype(jnp.float32)
        weight_total = weight_total + weight
        summed = summed + weight * spread(values[t * own : (t + 1) * own])
    heads_ref[...] = summed / weight_total
    columns = []
    for g in range(group):
        columns.append(
            jnp.concatenate(
                [
                    heads_ref[pl.ds(s * group + g, own, stride=rows), :]
                    for s in range(steps)
                ],
                axis=0,
            )
        )
    heads = jnp.concatenate(columns, axis=1).astype(jnp.bfloat16)
    for d in range(out_ref.shape[0]):
        out_ref[d] = heads


def output_kernel(core_ref, heads_ref, w_ref, keep_ref, send_ref):
    owners, rows, width = heads_ref.shape
    steps = 2
    own = rows // steps
    core = core_ref[0]
    heads = heads_ref[...].reshape(owners * rows, width)
    columns = w_ref.shape[1]
    chunk = min(columns, 256)
    for start in range(0, columns, chunk):
        lanes = slice(start, start + chunk)
        part = jnp.dot(heads, w_ref[:, lanes], preferred_element_type=jnp.float32)
        part = part.reshape(owners, rows, chunk)
        first = part[:, :own].reshape(owners * own, chunk)
        second = part[:, own:].reshape(owners * own, chunk)
        keep_ref[:, lanes] = jnp.where(core == 0, first, second)
        send_ref[:, lanes] = jnp.where(core == 0, second, first).astype(jnp.bfloat16)


def local(
    hidden_in,
    w_query,
    key_weight_matrix,
    value_weight_matrix,
    w_out,
    paged_key_cache,
    paged_value_cache,
    block_request,
    block_fill,
    positions,
):
    bf16, f32 = jnp.bfloat16, jnp.float32
    steps, requests, _ = hidden_in.shape
    group = w_query.shape[1] // HEAD_SIZE
    owners = lax.axis_size("kvp")
    own = requests // owners
    rows = steps * own
    flat = rows * group
    scaling = HEAD_SIZE ** (-0.5)
    blocks, slots, _ = paged_key_cache.shape
    out_columns = w_out.shape[1]

    def exchange(x):
        return lax.all_to_all(x, "kvp", 0, 0, tiled=True)

    tp = lax.axis_index("tp")
    core = tp % 2
    hidden_in, core = lax.optimization_barrier((hidden_in, core))
    columns = (group + 2) * HEAD_SIZE
    parts, row_slots = pl.pallas_call(
        project_kernel,
        out_shape=(
            jax.ShapeDtypeStruct((owners, rows, columns), bf16),
            jax.ShapeDtypeStruct((rows, HEAD_SIZE), f32),
        ),
        in_specs=[HBM] * 5,
        out_specs=(VMEM, VMEM),
        scratch_shapes=[
            pltpu.SMEM(positions.shape, jnp.int32),
            pltpu.VMEM(hidden_in.shape, bf16),
            pltpu.VMEM(w_query.shape, bf16),
            pltpu.VMEM(key_weight_matrix.shape, bf16),
            pltpu.VMEM(value_weight_matrix.shape, bf16),
            pltpu.SemaphoreType.DMA((5,)),
        ],
        compiler_params=params(),
    )(*in_hbm(positions, hidden_in, w_query, key_weight_matrix, value_weight_matrix))
    cosine, sine = rotation_tables(row_slots)
    parts, cosine, sine = lax.optimization_barrier((parts, cosine, sine))
    parts = exchange(parts)
    queries, own_queries, new_rows = pl.pallas_call(
        rotate_kernel,
        out_shape=(
            jax.ShapeDtypeStruct((owners, flat, HEAD_SIZE), bf16),
            jax.ShapeDtypeStruct((flat, HEAD_SIZE), bf16),
            jax.ShapeDtypeStruct((2, rows, HEAD_SIZE), bf16),
        ),
        in_specs=[VMEM] * 3 + [HBM] * 2,
        out_specs=(VMEM, VMEM, VMEM),
        scratch_shapes=[pltpu.VMEM((flat, HEAD_SIZE), f32)],
        compiler_params=params(),
    )(parts, cosine, sine, *in_hbm(paged_key_cache, paged_value_cache))
    queries = exchange(queries).reshape(requests, steps * group, HEAD_SIZE)

    batch = 16
    sums = (requests, steps * group, HEAD_SIZE)
    parts = pl.pallas_call(
        functools.partial(attention_kernel, scaling, batch),
        out_shape=jax.ShapeDtypeStruct((owners, flat + STAT_ROWS, HEAD_SIZE), bf16),
        in_specs=[SMEM, SMEM, VMEM, VMEM, VMEM],
        out_specs=VMEM,
        scratch_shapes=[pltpu.VMEM(sums, f32)] * 3,
        compiler_params=params(32),
    )(
        block_request,
        block_fill,
        queries,
        *in_vmem(paged_key_cache, paged_value_cache),
    )
    parts = exchange(parts)
    heads = pl.pallas_call(
        functools.partial(finish_kernel, scaling),
        out_shape=jax.ShapeDtypeStruct((owners, rows, group * HEAD_SIZE), bf16),
        in_specs=[VMEM] * 3,
        out_specs=VMEM,
        scratch_shapes=[pltpu.VMEM((flat, HEAD_SIZE), f32)],
        compiler_params=params(),
    )(parts, own_queries, new_rows)
    heads = exchange(heads)

    half = (owners * own, out_columns)
    keep, send = pl.pallas_call(
        output_kernel,
        out_shape=(jax.ShapeDtypeStruct(half, f32), jax.ShapeDtypeStruct(half, bf16)),
        in_specs=[SMEM, VMEM, VMEM],
        out_specs=(VMEM, VMEM),
        compiler_params=params(),
    )(core.reshape(1), heads, w_out)

    devices = lax.axis_size("tp")

    def swap(x, bits):
        return lax.ppermute(x, "tp", [(i, i ^ bits) for i in range(devices)])

    mine = (keep + swap(send, 1).astype(f32)).astype(bf16)
    others = [swap(mine, bits) for bits in (2, 6, 4)]
    near, across, far = (x.astype(f32) for x in others)
    mine = ((mine.astype(f32) + near) + (across + far)).astype(bf16)
    other = swap(mine, 1)
    return jnp.where(core == 0, jnp.stack([mine, other]), jnp.stack([other, mine]))


def solution(mesh):
    return jax.shard_map(
        local,
        mesh=mesh,
        in_specs=(
            P(None, None, "kvp"),
            P("kvp", "tp"),
            P("kvp", "tp"),
            P("kvp", "tp"),
            P("tp", "kvp"),
            P("kvp", None, "tp"),
            P("kvp", None, "tp"),
            P("kvp"),
            P("kvp"),
            P(),
        ),
        out_specs=P(None, None, "kvp"),
        check_vma=False,
    )
```

```python
import functools

import jax
import jax.numpy as jnp
from jax import lax
from jax.experimental import pallas as pl
from jax.experimental.pallas import tpu as pltpu
from jax.sharding import PartitionSpec as P

HEAD_SIZE = 128
STAT_ROWS = 16
PIECES = 3

floor_score = -1e30
rope_base = 500000.0
VMEM = pl.BlockSpec(memory_space=pltpu.VMEM)
SMEM = pl.BlockSpec(memory_space=pltpu.SMEM)
HBM = pl.BlockSpec(memory_space=pltpu.HBM)
NT = (((1,), (1,)), ((), ()))


def params(mib=24):
    return pltpu.CompilerParams(vmem_limit_bytes=mib * 1024 * 1024)


def in_hbm(*arrays):
    return [pltpu.with_memory_space_constraint(a, pltpu.HBM) for a in arrays]


def in_vmem(*arrays):
    return [pltpu.with_memory_space_constraint(a, pltpu.VMEM) for a in arrays]


def rotation_tables(slots):
    half = HEAD_SIZE // 2
    pair = jnp.arange(HEAD_SIZE, dtype=jnp.int32) % half
    inverse = rope_base ** (-(pair.astype(jnp.float32) * 2.0 / HEAD_SIZE))
    angles = slots * inverse
    return jnp.cos(angles), jnp.sin(angles)


def project_kernel(
    position_hbm,
    hidden_hbm,
    wq_hbm,
    wk_hbm,
    wv_hbm,
    out_ref,
    slot_ref,
    position_ref,
    hidden_ref,
    wq_ref,
    wk_ref,
    wv_ref,
    sems,
):
    steps, requests, width = hidden_ref.shape
    owners, rows, columns = out_ref.shape
    own = rows // steps
    sources = (position_hbm, hidden_hbm, wk_hbm, wv_hbm, wq_hbm)
    targets = (position_ref, hidden_ref, wk_ref, wv_ref, wq_ref)
    copies = [
        pltpu.make_async_copy(source, target, sems.at[i])
        for i, (source, target) in enumerate(zip(sources, targets))
    ]
    for copy in copies:
        copy.start()
    first = lax.axis_index("kvp") * own
    copies[0].wait()
    row = lax.broadcasted_iota(jnp.int32, (rows, HEAD_SIZE), 0)
    slots = jnp.zeros((rows, HEAD_SIZE), jnp.int32)
    for r in range(own):
        slots = jnp.where(row % own == r, position_ref[first + r], slots)
    slot_ref[...] = (slots + row // own).astype(jnp.float32)
    copies[1].wait()
    hidden = hidden_ref[...].reshape(steps * requests, width)
    queries = wq_ref.shape[1]
    starts = (queries, queries + wk_ref.shape[1], 0)
    for copy, ref, column in zip(copies[2:], targets[2:], starts):
        copy.wait()
        total = ref.shape[1]
        chunk = min(total, 256)
        for start in range(0, total, chunk):
            part = jnp.dot(
                hidden, ref[:, start : start + chunk], preferred_element_type=jnp.float32
            )
            split = [
                part[s * requests : (s + 1) * requests].reshape(owners, own, chunk)
                for s in range(steps)
            ]
            lanes = slice(column + start, column + start + chunk)
            out_ref[:, :, lanes] = jnp.concatenate(split, axis=1).astype(jnp.bfloat16)


def rotate_kernel(parts_ref, cos_ref, sin_ref, keys_hbm, values_hbm, q_ref, own_ref, new_ref, turned_ref):
    sources, rows, columns = parts_ref.shape
    steps = 2
    own = rows // steps
    group = columns // HEAD_SIZE - 2
    lane = lax.broadcasted_iota(jnp.int32, (rows, HEAD_SIZE), 1)
    cosine = cos_ref[...]
    sine = jnp.where(lane < HEAD_SIZE // 2, -sin_ref[...], sin_ref[...])

    def head(index):
        lanes = slice(index * HEAD_SIZE, (index + 1) * HEAD_SIZE)
        return jnp.sum(parts_ref[:, :, lanes].astype(jnp.float32), axis=0)

    def rope(x):
        return x * cosine + pltpu.roll(x, HEAD_SIZE // 2, 1) * sine

    for g in range(group):
        x = rope(head(g))
        for s in range(steps):
            turned_ref[pl.ds(s * group + g, own, stride=steps * group), :] = x[
                s * own : (s + 1) * own
            ]
    new_ref[0] = rope(head(group)).astype(jnp.bfloat16)
    new_ref[1] = head(group + 1).astype(jnp.bfloat16)
    queries = turned_ref[...].astype(jnp.bfloat16)
    own_ref[...] = queries
    for d in range(q_ref.shape[0]):
        q_ref[d] = queries


def pieces(x):
    out = []
    for _ in range(PIECES):
        part = x.astype(jnp.bfloat16).astype(jnp.float32)
        out.append(part)
        x = x - part
    return out


def attention_kernel(
    scaling,
    batch,
    request_ref,
    fill_ref,
    q_ref,
    k_ref,
    v_ref,
    out_ref,
    max_ref,
    total_ref,
    sum_ref,
):
    blocks, slots, _ = k_ref.shape
    requests, rows, _ = q_ref.shape
    groups = blocks // batch
    lanes = batch * rows

    max_ref[...] = jnp.full_like(max_ref, floor_score)
    total_ref[...] = jnp.zeros_like(total_ref)
    sum_ref[...] = jnp.zeros_like(sum_ref)

    slot = lax.broadcasted_iota(jnp.int32, (lanes, slots), 1)

    def score(g):
        first = g * batch
        return jnp.concatenate(
            [
                lax.dot_general(
                    q_ref[request_ref[first + b]],
                    k_ref[first + b],
                    NT,
                    preferred_element_type=jnp.float32,
                )
                for b in range(batch)
            ],
            axis=0,
        )

    def weigh(g, scores):
        first = g * batch
        fill = jnp.concatenate(
            [jnp.full((rows, 1), fill_ref[first + b], jnp.int32) for b in range(batch)], axis=0
        )
        scores = jnp.where(slot < fill, scores * scaling, floor_score)
        largest = jnp.max(scores, axis=1, keepdims=True)
        weights = jnp.exp(scores - largest).astype(jnp.bfloat16)
        total = jnp.sum(weights.astype(jnp.float32), axis=1, keepdims=True)
        summed = [
            jnp.dot(
                weights[b * rows : (b + 1) * rows],
                v_ref[first + b],
                preferred_element_type=jnp.float32,
            )
            for b in range(batch)
        ]
        return largest, total, summed

    def merge(g, largest, total, summed):
        for b in range(batch):
            mine = slice(b * rows, (b + 1) * rows)
            owner = request_ref[g * batch + b]
            before = max_ref[owner]
            after = jnp.maximum(before, largest[mine])
            keep = jnp.exp(before - after)
            add = jnp.exp(largest[mine] - after)
            max_ref[owner] = after
            total_ref[owner] = total_ref[owner] * keep + total[mine] * add
            sum_ref[owner] = sum_ref[owner] * keep + summed[b] * add

    scores = score(0)
    for g in range(groups):
        later = score(g + 1) if g + 1 < groups else None
        merge(g, *weigh(g, scores))
        scores = later

    owners = out_ref.shape[0]
    own = requests // owners
    flat = own * rows
    diagonal = lax.broadcasted_iota(jnp.int32, (flat, HEAD_SIZE), 0) == lax.broadcasted_iota(
        jnp.int32, (flat, HEAD_SIZE), 1
    )

    def by_lane(ref):
        return jnp.concatenate(
            [
                jnp.sum(
                    jnp.where(
                        diagonal, ref[d * own : (d + 1) * own].reshape(flat, HEAD_SIZE), 0.0
                    ),
                    axis=0,
                    keepdims=True,
                )
                for d in range(owners)
            ],
            axis=0,
        )

    values = pieces(by_lane(max_ref)) + pieces(by_lane(total_ref))
    empty = jnp.zeros((STAT_ROWS - len(values), HEAD_SIZE), jnp.float32)
    for d in range(owners):
        out_ref[d, :flat, :] = (
            sum_ref[d * own : (d + 1) * own].reshape(flat, HEAD_SIZE).astype(jnp.bfloat16)
        )
        out_ref[d, flat:, :] = jnp.concatenate(
            [value[d : d + 1] for value in values] + [empty], axis=0
        ).astype(jnp.bfloat16)


def finish_kernel(scaling, parts_ref, q_ref, new_ref, out_ref, heads_ref):
    sources = parts_ref.shape[0]
    flat = q_ref.shape[0]
    steps = 2
    own = new_ref.shape[1] // steps
    rows = flat // own
    group = rows // steps

    stats = parts_ref[:, flat:, :].astype(jnp.float32)
    largest = sum(stats[:, i, :] for i in range(PIECES))
    total = sum(stats[:, PIECES + i, :] for i in range(PIECES))
    pad = HEAD_SIZE - sources
    largest = jnp.concatenate([largest, jnp.full((pad, flat), floor_score, jnp.float32)], axis=0).T
    total = jnp.concatenate([total, jnp.zeros((pad, flat), jnp.float32)], axis=0).T

    def spread(x):
        return jnp.broadcast_to(x[:, None, :], (own, rows, HEAD_SIZE)).reshape(flat, HEAD_SIZE)

    queries = q_ref[...].astype(jnp.float32)
    keys = new_ref[0].astype(jnp.float32)
    values = new_ref[1].astype(jnp.float32)
    row = lax.broadcasted_iota(jnp.int32, (flat, 1), 0)
    row_step = (row % rows) // group
    scores = []
    for t in range(steps):
        score = (
            jnp.sum(queries * spread(keys[t * own : (t + 1) * own]), axis=1, keepdims=True)
            * scaling
        )
        scores.append(jnp.where(row_step >= t, score, floor_score))
    peak = jnp.max(largest, axis=1, keepdims=True)
    for score in scores:
        peak = jnp.maximum(peak, score)
    factor = jnp.exp(largest - peak)
    weight_total = jnp.sum(factor * total, axis=1, keepdims=True)
    summed = jnp.zeros((flat, HEAD_SIZE), jnp.float32)
    for source in range(sources):
        summed = summed + factor[:, source : source + 1] * parts_ref[source, :flat, :].astype(
            jnp.float32
        )
    for t in range(steps):
        weight = jnp.exp(scores[t] - peak).astype(jnp.bfloat16).astype(jnp.float32)
        weight_total = weight_total + weight
        summed = summed + weight * spread(values[t * own : (t + 1) * own])
    heads_ref[...] = summed / weight_total
    columns = []
    for g in range(group):
        columns.append(
            jnp.concatenate(
                [
                    heads_ref[pl.ds(s * group + g, own, stride=rows), :]
                    for s in range(steps)
                ],
                axis=0,
            )
        )
    heads = jnp.concatenate(columns, axis=1).astype(jnp.bfloat16)
    for d in range(out_ref.shape[0]):
        out_ref[d] = heads


def output_kernel(heads_ref, w_ref, out_ref):
    owners, rows, width = heads_ref.shape
    steps = out_ref.shape[0]
    own = rows // steps
    heads = heads_ref[...].reshape(owners * rows, width)
    columns = w_ref.shape[1]
    chunk = min(columns, 256)
    for start in range(0, columns, chunk):
        lanes = slice(start, start + chunk)
        part = jnp.dot(heads, w_ref[:, lanes], preferred_element_type=jnp.float32)
        part = part.reshape(owners, rows, chunk)
        for s in range(steps):
            out_ref[s, :, lanes] = (
                part[:, s * own : (s + 1) * own].reshape(owners * own, chunk).astype(jnp.bfloat16)
            )


def local(
    hidden_in,
    w_query,
    key_weight_matrix,
    value_weight_matrix,
    w_out,
    paged_key_cache,
    paged_value_cache,
    block_request,
    block_fill,
    positions,
):
    bf16, f32 = jnp.bfloat16, jnp.float32
    steps, requests, _ = hidden_in.shape
    group = w_query.shape[1] // HEAD_SIZE
    owners = lax.axis_size("kvp")
    own = requests // owners
    rows = steps * own
    flat = rows * group
    scaling = HEAD_SIZE ** (-0.5)
    blocks, slots, _ = paged_key_cache.shape
    out_columns = w_out.shape[1]

    def exchange(x):
        return lax.all_to_all(x, "kvp", 0, 0, tiled=True)

    columns = (group + 2) * HEAD_SIZE
    parts, row_slots = pl.pallas_call(
        project_kernel,
        out_shape=(
            jax.ShapeDtypeStruct((owners, rows, columns), bf16),
            jax.ShapeDtypeStruct((rows, HEAD_SIZE), f32),
        ),
        in_specs=[HBM] * 5,
        out_specs=(VMEM, VMEM),
        scratch_shapes=[
            pltpu.SMEM(positions.shape, jnp.int32),
            pltpu.VMEM(hidden_in.shape, bf16),
            pltpu.VMEM(w_query.shape, bf16),
            pltpu.VMEM(key_weight_matrix.shape, bf16),
            pltpu.VMEM(value_weight_matrix.shape, bf16),
            pltpu.SemaphoreType.DMA((5,)),
        ],
        compiler_params=params(),
    )(*in_hbm(positions, hidden_in, w_query, key_weight_matrix, value_weight_matrix))
    cosine, sine = rotation_tables(row_slots)
    parts, cosine, sine = lax.optimization_barrier((parts, cosine, sine))
    parts = exchange(parts)
    queries, own_queries, new_rows = pl.pallas_call(
        rotate_kernel,
        out_shape=(
            jax.ShapeDtypeStruct((owners, flat, HEAD_SIZE), bf16),
            jax.ShapeDtypeStruct((flat, HEAD_SIZE), bf16),
            jax.ShapeDtypeStruct((2, rows, HEAD_SIZE), bf16),
        ),
        in_specs=[VMEM] * 3 + [HBM] * 2,
        out_specs=(VMEM, VMEM, VMEM),
        scratch_shapes=[pltpu.VMEM((flat, HEAD_SIZE), f32)],
        compiler_params=params(),
    )(parts, cosine, sine, *in_hbm(paged_key_cache, paged_value_cache))
    queries = exchange(queries).reshape(requests, steps * group, HEAD_SIZE)

    batch = 16
    sums = (requests, steps * group, HEAD_SIZE)
    parts = pl.pallas_call(
        functools.partial(attention_kernel, scaling, batch),
        out_shape=jax.ShapeDtypeStruct((owners, flat + STAT_ROWS, HEAD_SIZE), bf16),
        in_specs=[SMEM, SMEM, VMEM, VMEM, VMEM],
        out_specs=VMEM,
        scratch_shapes=[pltpu.VMEM(sums, f32)] * 3,
        compiler_params=params(32),
    )(
        block_request,
        block_fill,
        queries,
        *in_vmem(paged_key_cache, paged_value_cache),
    )
    parts = exchange(parts)
    heads = pl.pallas_call(
        functools.partial(finish_kernel, scaling),
        out_shape=jax.ShapeDtypeStruct((owners, rows, group * HEAD_SIZE), bf16),
        in_specs=[VMEM] * 3,
        out_specs=VMEM,
        scratch_shapes=[pltpu.VMEM((flat, HEAD_SIZE), f32)],
        compiler_params=params(),
    )(parts, own_queries, new_rows)
    heads = exchange(heads)

    part = pl.pallas_call(
        output_kernel,
        out_shape=jax.ShapeDtypeStruct((steps, requests, out_columns), bf16),
        in_specs=[VMEM, VMEM],
        out_specs=VMEM,
        compiler_params=params(),
    )(heads, w_out)

    devices = lax.axis_size("tp")

    def swap(x, bits):
        return lax.ppermute(x, "tp", [(i, i ^ bits) for i in range(devices)])

    near, across, far = (swap(part, bits).astype(f32) for bits in (2, 6, 4))
    chips = ((part.astype(f32) + near) + (across + far)).astype(bf16)
    return (chips.astype(f32) + swap(chips, 1).astype(f32)).astype(bf16)


def solution(mesh):
    return jax.shard_map(
        local,
        mesh=mesh,
        in_specs=(
            P(None, None, "kvp"),
            P("kvp", "tp"),
            P("kvp", "tp"),
            P("kvp", "tp"),
            P("tp", "kvp"),
            P("kvp", None, "tp"),
            P("kvp", None, "tp"),
            P("kvp"),
            P("kvp"),
            P(),
        ),
        out_specs=P(None, None, "kvp"),
        check_vma=False,
    )
```

```python
import functools

import jax
import jax.numpy as jnp
from jax import lax
from jax.experimental import pallas as pl
from jax.experimental.pallas import tpu as pltpu
from jax.sharding import PartitionSpec as P

HEAD_SIZE = 128
STAT_ROWS = 16
PIECES = 3

floor_score = -1e30
rope_base = 500000.0
VMEM = pl.BlockSpec(memory_space=pltpu.VMEM)
SMEM = pl.BlockSpec(memory_space=pltpu.SMEM)
HBM = pl.BlockSpec(memory_space=pltpu.HBM)
NT = (((1,), (1,)), ((), ()))


def params(mib=24):
    return pltpu.CompilerParams(vmem_limit_bytes=mib * 1024 * 1024)


def in_hbm(*arrays):
    return [pltpu.with_memory_space_constraint(a, pltpu.HBM) for a in arrays]


def in_vmem(*arrays):
    return [pltpu.with_memory_space_constraint(a, pltpu.VMEM) for a in arrays]


def rotation_tables(slots):
    half = HEAD_SIZE // 2
    pair = jnp.arange(HEAD_SIZE, dtype=jnp.int32) % half
    inverse = rope_base ** (-(pair.astype(jnp.float32) * 2.0 / HEAD_SIZE))
    angles = slots * inverse
    return jnp.cos(angles), jnp.sin(angles)


def project_kernel(
    position_hbm,
    hidden_hbm,
    wq_hbm,
    wk_hbm,
    wv_hbm,
    out_ref,
    slot_ref,
    position_ref,
    hidden_ref,
    wq_ref,
    wk_ref,
    wv_ref,
    sems,
):
    steps, requests, width = hidden_ref.shape
    owners, rows, columns = out_ref.shape
    own = rows // steps
    sources = (position_hbm, hidden_hbm, wk_hbm, wv_hbm, wq_hbm)
    targets = (position_ref, hidden_ref, wk_ref, wv_ref, wq_ref)
    copies = [
        pltpu.make_async_copy(source, target, sems.at[i])
        for i, (source, target) in enumerate(zip(sources, targets))
    ]
    for copy in copies:
        copy.start()
    copies[1].wait()
    hidden = hidden_ref[...].reshape(steps * requests, width)
    queries = wq_ref.shape[1]
    starts = (queries, queries + wk_ref.shape[1], 0)
    for copy, ref, column in zip(copies[2:], targets[2:], starts):
        if ref is wq_ref:
            first = lax.axis_index("kvp") * own
            copies[0].wait()
            row = lax.broadcasted_iota(jnp.int32, (rows, HEAD_SIZE), 0)
            slots = jnp.zeros((rows, HEAD_SIZE), jnp.int32)
            for r in range(own):
                slots = jnp.where(row % own == r, position_ref[first + r], slots)
            slot_ref[...] = (slots + row // own).astype(jnp.float32)
        copy.wait()
        total = ref.shape[1]
        chunk = min(total, 256)
        for start in range(0, total, chunk):
            part = jnp.dot(
                hidden, ref[:, start : start + chunk], preferred_element_type=jnp.float32
            )
            split = [
                part[s * requests : (s + 1) * requests].reshape(owners, own, chunk)
                for s in range(steps)
            ]
            lanes = slice(column + start, column + start + chunk)
            out_ref[:, :, lanes] = jnp.concatenate(split, axis=1).astype(jnp.bfloat16)


def rotate_kernel(parts_ref, cos_ref, sin_ref, keys_hbm, values_hbm, q_ref, own_ref, new_ref, turned_ref):
    sources, rows, columns = parts_ref.shape
    steps = 2
    own = rows // steps
    group = columns // HEAD_SIZE - 2
    lane = lax.broadcasted_iota(jnp.int32, (rows, HEAD_SIZE), 1)
    cosine = cos_ref[...]
    sine = jnp.where(lane < HEAD_SIZE // 2, -sin_ref[...], sin_ref[...])

    def head(index):
        lanes = slice(index * HEAD_SIZE, (index + 1) * HEAD_SIZE)
        return jnp.sum(parts_ref[:, :, lanes].astype(jnp.float32), axis=0)

    def rope(x):
        return x * cosine + pltpu.roll(x, HEAD_SIZE // 2, 1) * sine

    for g in range(group):
        x = rope(head(g))
        for s in range(steps):
            turned_ref[pl.ds(s * group + g, own, stride=steps * group), :] = x[
                s * own : (s + 1) * own
            ]
    new_ref[0] = rope(head(group)).astype(jnp.bfloat16)
    new_ref[1] = head(group + 1).astype(jnp.bfloat16)
    queries = turned_ref[...].astype(jnp.bfloat16)
    own_ref[...] = queries
    for d in range(q_ref.shape[0]):
        q_ref[d] = queries


def pieces(x):
    out = []
    for _ in range(PIECES):
        part = x.astype(jnp.bfloat16).astype(jnp.float32)
        out.append(part)
        x = x - part
    return out


def attention_kernel(
    scaling,
    batch,
    request_ref,
    fill_ref,
    q_ref,
    k_ref,
    v_ref,
    out_ref,
    max_ref,
    total_ref,
    sum_ref,
):
    blocks, slots, _ = k_ref.shape
    requests, rows, _ = q_ref.shape
    groups = blocks // batch
    lanes = batch * rows

    max_ref[...] = jnp.full_like(max_ref, floor_score)
    total_ref[...] = jnp.zeros_like(total_ref)
    sum_ref[...] = jnp.zeros_like(sum_ref)

    slot = lax.broadcasted_iota(jnp.int32, (lanes, slots), 1)

    def score(g):
        first = g * batch
        return jnp.concatenate(
            [
                lax.dot_general(
                    q_ref[request_ref[first + b]],
                    k_ref[first + b],
                    NT,
                    preferred_element_type=jnp.float32,
                )
                for b in range(batch)
            ],
            axis=0,
        )

    def weigh(g, scores):
        first = g * batch
        fill = jnp.concatenate(
            [jnp.full((rows, 1), fill_ref[first + b], jnp.int32) for b in range(batch)], axis=0
        )
        scores = jnp.where(slot < fill, scores * scaling, floor_score)
        largest = jnp.max(scores, axis=1, keepdims=True)
        weights = jnp.exp(scores - largest).astype(jnp.bfloat16)
        total = jnp.sum(weights.astype(jnp.float32), axis=1, keepdims=True)
        summed = [
            jnp.dot(
                weights[b * rows : (b + 1) * rows],
                v_ref[first + b],
                preferred_element_type=jnp.float32,
            )
            for b in range(batch)
        ]
        return largest, total, summed

    def merge(g, largest, total, summed):
        for b in range(batch):
            mine = slice(b * rows, (b + 1) * rows)
            owner = request_ref[g * batch + b]
            before = max_ref[owner]
            after = jnp.maximum(before, largest[mine])
            keep = jnp.exp(before - after)
            add = jnp.exp(largest[mine] - after)
            max_ref[owner] = after
            total_ref[owner] = total_ref[owner] * keep + total[mine] * add
            sum_ref[owner] = sum_ref[owner] * keep + summed[b] * add

    scores = score(0)
    for g in range(groups):
        later = score(g + 1) if g + 1 < groups else None
        merge(g, *weigh(g, scores))
        scores = later

    owners = out_ref.shape[0]
    own = requests // owners
    flat = own * rows
    diagonal = lax.broadcasted_iota(jnp.int32, (flat, HEAD_SIZE), 0) == lax.broadcasted_iota(
        jnp.int32, (flat, HEAD_SIZE), 1
    )

    def by_lane(ref):
        return jnp.concatenate(
            [
                jnp.sum(
                    jnp.where(
                        diagonal, ref[d * own : (d + 1) * own].reshape(flat, HEAD_SIZE), 0.0
                    ),
                    axis=0,
                    keepdims=True,
                )
                for d in range(owners)
            ],
            axis=0,
        )

    values = pieces(by_lane(max_ref)) + pieces(by_lane(total_ref))
    empty = jnp.zeros((STAT_ROWS - len(values), HEAD_SIZE), jnp.float32)
    for d in range(owners):
        out_ref[d, :flat, :] = (
            sum_ref[d * own : (d + 1) * own].reshape(flat, HEAD_SIZE).astype(jnp.bfloat16)
        )
        out_ref[d, flat:, :] = jnp.concatenate(
            [value[d : d + 1] for value in values] + [empty], axis=0
        ).astype(jnp.bfloat16)


def finish_kernel(scaling, parts_ref, q_ref, new_ref, out_ref, heads_ref):
    sources = parts_ref.shape[0]
    flat = q_ref.shape[0]
    steps = 2
    own = new_ref.shape[1] // steps
    rows = flat // own
    group = rows // steps

    stats = parts_ref[:, flat:, :].astype(jnp.float32)
    largest = sum(stats[:, i, :] for i in range(PIECES))
    total = sum(stats[:, PIECES + i, :] for i in range(PIECES))
    pad = HEAD_SIZE - sources
    largest = jnp.concatenate([largest, jnp.full((pad, flat), floor_score, jnp.float32)], axis=0).T
    total = jnp.concatenate([total, jnp.zeros((pad, flat), jnp.float32)], axis=0).T

    def spread(x):
        return jnp.broadcast_to(x[:, None, :], (own, rows, HEAD_SIZE)).reshape(flat, HEAD_SIZE)

    queries = q_ref[...].astype(jnp.float32)
    keys = new_ref[0].astype(jnp.float32)
    values = new_ref[1].astype(jnp.float32)
    row = lax.broadcasted_iota(jnp.int32, (flat, 1), 0)
    row_step = (row % rows) // group
    scores = []
    for t in range(steps):
        score = (
            jnp.sum(queries * spread(keys[t * own : (t + 1) * own]), axis=1, keepdims=True)
            * scaling
        )
        scores.append(jnp.where(row_step >= t, score, floor_score))
    peak = jnp.max(largest, axis=1, keepdims=True)
    for score in scores:
        peak = jnp.maximum(peak, score)
    factor = jnp.exp(largest - peak)
    weight_total = jnp.sum(factor * total, axis=1, keepdims=True)
    summed = jnp.zeros((flat, HEAD_SIZE), jnp.float32)
    for source in range(sources):
        summed = summed + factor[:, source : source + 1] * parts_ref[source, :flat, :].astype(
            jnp.float32
        )
    for t in range(steps):
        weight = jnp.exp(scores[t] - peak).astype(jnp.bfloat16).astype(jnp.float32)
        weight_total = weight_total + weight
        summed = summed + weight * spread(values[t * own : (t + 1) * own])
    heads_ref[...] = summed / weight_total
    columns = []
    for g in range(group):
        columns.append(
            jnp.concatenate(
                [
                    heads_ref[pl.ds(s * group + g, own, stride=rows), :]
                    for s in range(steps)
                ],
                axis=0,
            )
        )
    heads = jnp.concatenate(columns, axis=1).astype(jnp.bfloat16)
    for d in range(out_ref.shape[0]):
        out_ref[d] = heads


def output_kernel(heads_ref, w_ref, out_ref):
    owners, rows, width = heads_ref.shape
    steps = out_ref.shape[0]
    own = rows // steps
    heads = heads_ref[...].reshape(owners * rows, width)
    columns = w_ref.shape[1]
    chunk = min(columns, 256)
    for start in range(0, columns, chunk):
        lanes = slice(start, start + chunk)
        part = jnp.dot(heads, w_ref[:, lanes], preferred_element_type=jnp.float32)
        part = part.reshape(owners, rows, chunk)
        for s in range(steps):
            out_ref[s, :, lanes] = (
                part[:, s * own : (s + 1) * own].reshape(owners * own, chunk).astype(jnp.bfloat16)
            )


def local(
    hidden_in,
    w_query,
    key_weight_matrix,
    value_weight_matrix,
    w_out,
    paged_key_cache,
    paged_value_cache,
    block_request,
    block_fill,
    positions,
):
    bf16, f32 = jnp.bfloat16, jnp.float32
    steps, requests, _ = hidden_in.shape
    group = w_query.shape[1] // HEAD_SIZE
    owners = lax.axis_size("kvp")
    own = requests // owners
    rows = steps * own
    flat = rows * group
    scaling = HEAD_SIZE ** (-0.5)
    blocks, slots, _ = paged_key_cache.shape
    out_columns = w_out.shape[1]

    def exchange(x):
        return lax.all_to_all(x, "kvp", 0, 0, tiled=True)

    columns = (group + 2) * HEAD_SIZE
    parts, row_slots = pl.pallas_call(
        project_kernel,
        out_shape=(
            jax.ShapeDtypeStruct((owners, rows, columns), bf16),
            jax.ShapeDtypeStruct((rows, HEAD_SIZE), f32),
        ),
        in_specs=[HBM] * 5,
        out_specs=(VMEM, VMEM),
        scratch_shapes=[
            pltpu.SMEM(positions.shape, jnp.int32),
            pltpu.VMEM(hidden_in.shape, bf16),
            pltpu.VMEM(w_query.shape, bf16),
            pltpu.VMEM(key_weight_matrix.shape, bf16),
            pltpu.VMEM(value_weight_matrix.shape, bf16),
            pltpu.SemaphoreType.DMA((5,)),
        ],
        compiler_params=params(),
    )(*in_hbm(positions, hidden_in, w_query, key_weight_matrix, value_weight_matrix))
    cosine, sine = rotation_tables(row_slots)
    parts, cosine, sine = lax.optimization_barrier((parts, cosine, sine))
    parts = exchange(parts)
    queries, own_queries, new_rows = pl.pallas_call(
        rotate_kernel,
        out_shape=(
            jax.ShapeDtypeStruct((owners, flat, HEAD_SIZE), bf16),
            jax.ShapeDtypeStruct((flat, HEAD_SIZE), bf16),
            jax.ShapeDtypeStruct((2, rows, HEAD_SIZE), bf16),
        ),
        in_specs=[VMEM] * 3 + [HBM] * 2,
        out_specs=(VMEM, VMEM, VMEM),
        scratch_shapes=[pltpu.VMEM((flat, HEAD_SIZE), f32)],
        compiler_params=params(),
    )(parts, cosine, sine, *in_hbm(paged_key_cache, paged_value_cache))
    queries = exchange(queries).reshape(requests, steps * group, HEAD_SIZE)

    batch = 16
    sums = (requests, steps * group, HEAD_SIZE)
    parts = pl.pallas_call(
        functools.partial(attention_kernel, scaling, batch),
        out_shape=jax.ShapeDtypeStruct((owners, flat + STAT_ROWS, HEAD_SIZE), bf16),
        in_specs=[SMEM, SMEM, VMEM, VMEM, VMEM],
        out_specs=VMEM,
        scratch_shapes=[pltpu.VMEM(sums, f32)] * 3,
        compiler_params=params(32),
    )(
        block_request,
        block_fill,
        queries,
        *in_vmem(paged_key_cache, paged_value_cache),
    )
    parts = exchange(parts)
    heads = pl.pallas_call(
        functools.partial(finish_kernel, scaling),
        out_shape=jax.ShapeDtypeStruct((owners, rows, group * HEAD_SIZE), bf16),
        in_specs=[VMEM] * 3,
        out_specs=VMEM,
        scratch_shapes=[pltpu.VMEM((flat, HEAD_SIZE), f32)],
        compiler_params=params(),
    )(parts, own_queries, new_rows)
    heads = exchange(heads)

    part = pl.pallas_call(
        output_kernel,
        out_shape=jax.ShapeDtypeStruct((steps, requests, out_columns), bf16),
        in_specs=[VMEM, VMEM],
        out_specs=VMEM,
        compiler_params=params(),
    )(heads, w_out)

    devices = lax.axis_size("tp")

    def swap(x, bits):
        return lax.ppermute(x, "tp", [(i, i ^ bits) for i in range(devices)])

    near, across, far = (swap(part, bits).astype(f32) for bits in (2, 6, 4))
    chips = ((part.astype(f32) + near) + (across + far)).astype(bf16)
    return (chips.astype(f32) + swap(chips, 1).astype(f32)).astype(bf16)


def solution(mesh):
    return jax.shard_map(
        local,
        mesh=mesh,
        in_specs=(
            P(None, None, "kvp"),
            P("kvp", "tp"),
            P("kvp", "tp"),
            P("kvp", "tp"),
            P("tp", "kvp"),
            P("kvp", None, "tp"),
            P("kvp", None, "tp"),
            P("kvp"),
            P("kvp"),
            P(),
        ),
        out_specs=P(None, None, "kvp"),
        check_vma=False,
    )
```
